512 devices in a mesh: dp: 8 (over x, core), expert: 64 (over z, y).
Axes of the slice: x: 4, y: 4, z: 16, core: 2. Of those that a mesh axis runs over, the one named last changes fastest.
Arguments:
- tokens: bfloat16 [4096, 2048], P(('dp', 'expert')), may hold values from -6 to 6
- out_grad: bfloat16 [4096, 2048], P(('dp', 'expert')), may hold values from -6 to 6
- expert_ids: int32 [4096, 8], P(('dp', 'expert')), may hold values from 0 to 63, all different within a row; in each aligned block of 8 rows (0 to 7, 8 to 15, ...) at most 2 rows name the same one
- gate_values: float32 [4096, 8], P(('dp', 'expert')), may hold values from 0.05 to 1
- w_gate: bfloat16 [64, 2048, 1024], P('expert', None, 'dp'), may hold values from -0.125 to 0.125
- w_up: bfloat16 [64, 2048, 1024], P('expert', None, 'dp'), may hold values from -0.125 to 0.125
- w_down: bfloat16 [64, 1024, 2048], P('expert', 'dp'), may hold values from -0.1875 to 0.1875
Outputs:
- grad_tokens: bfloat16 [4096, 2048], P(('dp', 'expert'))
- grad_gate: float32 [64, 2048, 1024], P('expert', None, 'dp')
- grad_up: float32 [64, 2048, 1024], P('expert', None, 'dp')
- grad_down: float32 [64, 1024, 2048], P('expert', 'dp')
The draws below stay inside these ranges and needn't reach their ends.
Inputs may be any that keep to these rules, and one draw needn't show every extreme that they name: `expert_ids`: each token names 8 different experts. Among the 8 tokens of one device (aligned blocks of 8 rows) no expert is named more than 2 times, and in every draw some expert is named exactly 2 times in some block.
All inputs are finite; a program needn't handle non-finite values.
Results may differ from the reference program's by a relative error of at most 0.014.
Values may be sent and summed in bfloat16 or wider, within the bound.
A program may use at most 64 MiB of HBM per device.

```python
import math
import jax
import jax.numpy as jnp
import numpy as np
from jax import lax

D = 2048
FF = 1024
TOP = 8
TOK_DEV = 8
EXPERTS = 64
CAP = 2
ROWS = 1024
TOKENS = 4096
N_DP = 8
N_EXPERT = 64


def steps_of(stream_key, extent, split, least, high):
    def one(dim, blocks):
        heights = jax.random.uniform(jax.random.fold_in(jax.random.fold_in(stream_key, 6), dim), (blocks,), jnp.float32, least / len(split), high / len(split))
        return jnp.repeat(jnp.exp(heights), extent[dim] // blocks).reshape((-1,) + (1,) * (len(extent) - dim - 1))

    factor_of = one(*split[0])
    for cut in split[1:]:
        factor_of = factor_of * one(*cut)
    return factor_of


def routed_block(own_key, own, number, rows, count, top, limit, lean):
    order = jax.random.permutation(own_key, count)
    heavy_load, ordinary = shares(count, rows * top, limit, lean, True), shares(count, rows * top, limit, lean, False)
    places = jnp.arange(count)

    def named(lengths, offset_by):
        used = int((lengths > 0).sum())
        fixed = max(1, used // 4)
        passed = fixed + (places - fixed + offset_by * (used - fixed)) % max(1, count - fixed)
        return jnp.zeros((count,), jnp.int32).at[order[jnp.where(places < fixed, places, passed)]].set(jnp.asarray(lengths, jnp.int32))

    lengths = jnp.where(number % 4 == 0, named(heavy_load, number // 4), named(ordinary, number - number // 4 - 1))
    mixed = jax.random.permutation(jax.random.fold_in(own, 3), count)
    donor, receiver = mixed[0:count // 2 * 2:2], mixed[1:count // 2 * 2:2]
    slack = jnp.minimum(lengths[donor] - 1, limit - lengths[receiver]) // 2
    slack = jnp.where((donor == order[0]) | (receiver == order[0]) | (lengths[receiver] == 0), 0, jnp.maximum(slack, 0))
    passed = jax.random.randint(jax.random.fold_in(own, 4), (count // 2,), 0, 1 << 20) % (slack + 1)
    lengths = lengths.at[donor].add(-passed).at[receiver].add(passed)
    items = jnp.searchsorted(jnp.cumsum(lengths), jnp.arange(rows * top), side="right").astype(jnp.int32)
    grid = items.reshape(top, rows).T
    grid = grid[jax.random.permutation(jax.random.fold_in(own, 1), rows)]
    offset_by = jax.random.randint(jax.random.fold_in(own, 2), (rows, 1), 0, top)
    return jnp.take_along_axis(grid, (jnp.arange(top)[None, :] + offset_by) % top, axis=1)


def shares(count, total, limit, slope, full):
    loads = [(1 << 20) // math.isqrt(grade ** slope) + 1 for grade in range(1, count + 1)]
    largest = limit if full else min(limit, max(-(-total // count), total * loads[0] // sum(loads)))
    least = 1 if total - largest >= count - 1 else 0
    given, spare = [largest] + [least] * (count - 1), total - largest - least * (count - 1)
    while spare > 0:
        free = [i for i in range(1, count) if given[i] < largest] or [i for i in range(1, count) if given[i] < limit]
        pool, budget = sum([loads[i] for i in free]), spare
        for i in free:
            addition = min(limit - given[i], max(1, budget * loads[i] // pool), spare)
            given[i] = given[i] + addition
            spare = spare - addition
    return np.array(given)


def scatter_about(rng, shape, scale, most, pieces=(), held_as=jnp.bfloat16):
    drawn = scale * jax.random.normal(rng, shape, jnp.float32)
    if pieces:
        drawn = drawn * steps_of(rng, shape, pieces, -0.22, 0.18)
    return jnp.clip(drawn, -most, most).astype(held_as)


def setup_inputs(seed: int = 0) -> dict:
    splits = jax.random.split(jax.random.key(seed), 8)
    tokens = scatter_about(splits[0], (TOKENS, D), 1.0, 6.0, ((0, 512),))
    out_grad = scatter_about(splits[1], (TOKENS, D), 1.0, 6.0, ((0, 512),))
    expert_ids_keys = jax.random.split(jax.random.fold_in(splits[2], 1), TOKENS // TOK_DEV)
    expert_ids_turns = jax.random.permutation(jax.random.fold_in(splits[2], 3), TOKENS // TOK_DEV)
    expert_ids = jax.vmap(lambda own, number: routed_block(jax.random.fold_in(splits[2], 2), own, number, TOK_DEV, EXPERTS, TOP, CAP, 2))(expert_ids_keys, expert_ids_turns).reshape((TOKENS, TOP))
    gate_values = jnp.clip(0.05 + 0.95 * jax.random.uniform(splits[3], (TOKENS, TOP), jnp.float32) ** steps_of(splits[3], (TOKENS, TOP), ((0, 512),), -0.2, 0.2), 0.05, 1.0)
    w_gate = scatter_about(splits[4], (EXPERTS, D, FF), D ** -0.5, 0.125, ((0, 64), (2, 8)))
    w_up = scatter_about(splits[5], (EXPERTS, D, FF), D ** -0.5, 0.125, ((0, 64), (2, 8)))
    w_down = scatter_about(splits[6], (EXPERTS, FF, D), FF ** -0.5, 0.1875, ((0, 64), (1, 8)))
    return {"tokens": tokens, "out_grad": out_grad, "expert_ids": expert_ids, "gate_values": gate_values, "w_gate": w_gate, "w_up": w_up, "w_down": w_down}


def reference(tokens, out_grad, expert_ids, gate_values, w_gate, w_up, w_down):
    blocks = TOKENS // TOK_DEV
    id_blocks = expert_ids.reshape(blocks, TOK_DEV * TOP)
    onehot = (id_blocks[:, :, None] == jnp.arange(EXPERTS, dtype=jnp.int32)[None, None, :]).astype(jnp.int32)
    before = jnp.cumsum(onehot, axis=1) - onehot
    slot_rank = jnp.sum(before * onehot, axis=2).astype(jnp.int32)
    block_index = jnp.arange(blocks, dtype=jnp.int32)[:, None]
    batch_index = block_index // N_EXPERT
    source_index = block_index % N_EXPERT
    position = id_blocks * ROWS + (batch_index * N_EXPERT + source_index) * CAP + slot_rank
    token_index = block_index * TOK_DEV + (jnp.arange(TOK_DEV * TOP, dtype=jnp.int32) // TOP)[None, :]
    token_index = jnp.broadcast_to(token_index, position.shape).astype(jnp.int32)
    table = jnp.full((EXPERTS * ROWS,), TOKENS, dtype=jnp.int32)
    table = table.at[position.reshape(-1)].set(token_index.reshape(-1)).reshape(EXPERTS, ROWS)
    gate_table = jnp.zeros((EXPERTS * ROWS,), dtype=jnp.float32)
    gate_table = gate_table.at[position.reshape(-1)].set(gate_values.reshape(-1)).reshape(EXPERTS, ROWS)
    tokens_pad = jnp.concatenate([tokens, jnp.zeros((1, D), dtype=tokens.dtype)], axis=0)
    grads_pad = jnp.concatenate([out_grad, jnp.zeros((1, D), dtype=out_grad.dtype)], axis=0)
    block_width = FF // N_DP

    def one_expert(operands):
        index_row, gate_row, weight_gate, weight_up, weight_down = operands
        x_rows = tokens_pad[index_row]
        g_rows = (gate_row[:, None] * grads_pad[index_row].astype(jnp.float32)).astype(jnp.bfloat16)
        gate_pre = jnp.dot(x_rows, weight_gate, preferred_element_type=jnp.float32)
        up_pre = jnp.dot(x_rows, weight_up, preferred_element_type=jnp.float32)
        sigmoid_val = jax.nn.sigmoid(gate_pre)
        silu_val = gate_pre * sigmoid_val
        activation = (silu_val * up_pre).astype(jnp.bfloat16)
        act_grad = jnp.dot(g_rows, weight_down.T, preferred_element_type=jnp.float32)
        up_grad = (act_grad * silu_val).astype(jnp.bfloat16)
        gate_grad = (act_grad * up_pre * sigmoid_val * (1.0 + gate_pre * (1.0 - sigmoid_val))).astype(jnp.bfloat16)
        grad_g = jnp.dot(x_rows.T, gate_grad, preferred_element_type=jnp.float32)
        grad_u = jnp.dot(x_rows.T, up_grad, preferred_element_type=jnp.float32)
        grad_d = jnp.dot(activation.T, g_rows, preferred_element_type=jnp.float32)
        row_sums = jnp.zeros((ROWS, D), dtype=jnp.float32)
        for block in range(N_DP):
            low = block * block_width
            high = low + block_width
            term = jnp.dot(gate_grad[:, low:high], weight_gate[:, low:high].T, preferred_element_type=jnp.float32)
            term = term + jnp.dot(up_grad[:, low:high], weight_up[:, low:high].T, preferred_element_type=jnp.float32)
            rounded = lax.optimization_barrier(term.astype(jnp.bfloat16))
            row_sums = row_sums + rounded.astype(jnp.float32)
        return grad_g, grad_u, grad_d, row_sums

    grad_gate, grad_up, grad_down, row_grads = lax.map(one_expert, (table, gate_table, w_gate, w_up, w_down))
    summed = jnp.zeros((TOKENS + 1, D), dtype=jnp.float32)
    summed = summed.at[table.reshape(-1)].add(row_grads.reshape(EXPERTS * ROWS, D))
    grad_tokens = summed[:TOKENS].astype(jnp.bfloat16)
    return grad_tokens, grad_gate, grad_up, grad_down
```

```python
import jax
import jax.numpy as jnp
from jax import lax
from jax.sharding import PartitionSpec as P

NZ, NY, CAP = 16, 4, 2
BF, F32 = jnp.bfloat16, jnp.float32


def contract_last(a, b):
    return lax.dot_general(a, b, (((1,), (1,)), ((), ())), preferred_element_type=F32)


def contract_first(a, b):
    return lax.dot_general(a, b, (((0,), (0,)), ((), ())), preferred_element_type=F32)


def slot_table(ids, gates):
    rows = ids.shape[0]
    col = jnp.arange(128, dtype=jnp.int32)
    hit = ids[:, :, None] == (col // CAP)[None, None, :]
    gate = jnp.sum(jnp.where(hit, gates[:, :, None], 0.0), axis=1)
    used = (gate > 0.0).astype(jnp.int32)
    t = jnp.arange(rows)
    earlier = (t[:, None] > t[None, :]).astype(jnp.int32)
    rank = jnp.sum(earlier[:, :, None] * used[None, :, :], axis=1)
    return jnp.where(rank == (col % CAP)[None, :], gate, 0.0)


def shards(tokens, out_grad, ids, gates, w_gate, w_up, w_down):
    zg = [[NY * z + y for z in range(NZ)] for y in range(NY)]
    yg = [[NY * z + y for y in range(NY)] for z in range(NZ)]
    n, d = tokens.shape
    table = slot_table(ids, gates)
    both = jnp.concatenate([tokens, out_grad], axis=0)
    allb = lax.all_gather(both, "expert", axis_index_groups=zg)
    allt = lax.all_gather(table, "expert", axis_index_groups=zg)
    z = lax.axis_index("expert") // NY
    mine = lax.dynamic_slice_in_dim(allt, z * NY * CAP, NY * CAP, axis=2)
    mine = mine.reshape(NZ, n, NY, CAP)
    picks = (mine > 0.0).astype(BF)
    gate = jnp.sum(mine, axis=1)
    x = jnp.einsum("btys,btd->ybsd", picks, allb[:, :n], preferred_element_type=F32).astype(BF)
    g = jnp.einsum("btys,btd->ybsd", picks, allb[:, n:], preferred_element_type=F32)
    g = (g * gate.transpose(1, 0, 2)[..., None]).astype(BF)
    rows = NZ * CAP
    xg = jnp.stack([x.reshape(NY, rows, d), g.reshape(NY, rows, d)], axis=1)
    xg = lax.all_to_all(xg, "expert", 0, 0, axis_index_groups=yg, tiled=True)
    xg = lax.all_gather(xg, "dp")
    ndp = xg.shape[0]
    total = ndp * NY * rows
    x = xg[:, :, 0].reshape(total, d)
    g = xg[:, :, 1].reshape(total, d)
    wg, wu, wd = w_gate[0], w_up[0], w_down[0]
    gate_pre = jnp.dot(x, wg, preferred_element_type=F32)
    up_pre = jnp.dot(x, wu, preferred_element_type=F32)
    sig = jax.nn.sigmoid(gate_pre)
    silu = gate_pre * sig
    act = (silu * up_pre).astype(BF)
    act_grad = contract_last(g, wd)
    up_grad = (act_grad * silu).astype(BF)
    gate_grad = (act_grad * up_pre * sig * (1.0 + gate_pre * (1.0 - sig))).astype(BF)
    term = (contract_last(gate_grad, wg) + contract_last(up_grad, wu)).astype(BF)
    back = lax.psum_scatter(term.reshape(ndp, NY, rows, d), "dp", scatter_dimension=0)
    back = lax.all_to_all(back, "expert", 0, 0, axis_index_groups=yg, tiled=True)
    back = back.reshape(NY, NZ, CAP, d)
    sums = jnp.einsum("btys,ybsd->btd", picks, back, preferred_element_type=F32).astype(BF)
    grad_tokens = lax.psum_scatter(sums, "expert", scatter_dimension=0, axis_index_groups=zg)
    return (
        grad_tokens.astype(BF),
        contract_first(x, gate_grad)[None],
        contract_first(x, up_grad)[None],
        contract_first(act, g)[None],
    )


def solution(mesh):
    tok = P(("dp", "expert"), None)
    col, row = P("expert", None, "dp"), P("expert", "dp", None)
    return jax.shard_map(
        shards,
        mesh=mesh,
        in_specs=(tok, tok, tok, tok, col, col, row),
        out_specs=(tok, col, col, row),
        check_vma=False,
    )
```

```python
import jax
import jax.numpy as jnp
from jax import lax
from jax.experimental import pallas as pl
from jax.experimental.pallas import tpu as pltpu
from jax.sharding import PartitionSpec as P

BF, F32, I32 = jnp.bfloat16, jnp.float32, jnp.int32
NX, NY, NZ = 4, 4, 16
TOK, TOP, D, HID = 8, 8, 2048, 128
HALF = D // 2
R = {0: 0, 1: 1, 2: 2, 3: 3, 4: 4, 5: 8, 6: 9, 7: 10, 8: 11}
L = {0: 0, 1: 5, 2: 6, 3: 7, 4: 12, 5: 13, 6: 14, 7: 15}


def contract_last(a, b):
    return lax.dot_general(a, b, (((1,), (1,)), ((), ())), preferred_element_type=F32)


def contract_first(a, b):
    return lax.dot_general(a, b, (((0,), (0,)), ((), ())), preferred_element_type=F32)


def kernel(
    ids_ref, gates_ref, tok_ref, og_ref, wg_hbm, wu_hbm, wd_hbm,
    gtok_ref, gg_ref, gu_ref, gd_ref,
    table, tt, zbuf, picks, bsend, xg, wp, wd, pg, act, term, cbuf, pbuf, dbuf, ebuf,
    fbuf, rbuf, part, sbuf, nbuf, hbuf,
    wsem, az_s, az_r, at_s, at_r, y_s, y_r, x_s, x_r, k_s, k_r, c_s, c_r,
    d_s, d_r, e_s, e_r, f_s, f_r, n_s, n_r, h_s, h_r,
):
    dp, ex = lax.axis_index("dp"), lax.axis_index("expert")
    x, c = lax.div(dp, 2), lax.rem(dp, 2)
    z, y = lax.div(ex, NY), lax.rem(ex, NY)

    def at_z(k):
        return (dp, lax.rem(z + k + NZ, NZ) * NY + y)

    def at_y(k):
        return (dp, z * NY + lax.rem(y + k, NY))

    def at_x(k):
        return (lax.rem(x + k + NX, NX) * 2 + c, ex)

    sibling = (x * 2 + 1 - c, ex)
    started = []

    def remote(src, dst, ss, rs, device):
        copy = pltpu.make_async_remote_copy(
            src_ref=src, dst_ref=dst, send_sem=ss, recv_sem=rs,
            device_id=device, device_id_type=pl.DeviceIdType.MESH,
        )
        copy.start()
        started.append(copy)
        return copy

    barrier = pltpu.get_barrier_semaphore()
    others = [at_z(k) for k in (1, 2, 3, 4, 5, -1, -2, -3, -4, -5)]
    others += [at_y(k) for k in (1, 2, 3)] + [at_x(1), at_x(-1), sibling]
    for device in others:
        pl.semaphore_signal(barrier, inc=1, device_id=device, device_id_type=pl.DeviceIdType.MESH)

    loads = [
        pltpu.make_async_copy(wg_hbm, wp.at[:, 0:HID], wsem.at[0]),
        pltpu.make_async_copy(wu_hbm, wp.at[:, HID : 2 * HID], wsem.at[1]),
        pltpu.make_async_copy(wd_hbm, wd, wsem.at[2]),
    ]
    for load in loads:
        load.start()

    zbuf[0] = jnp.concatenate([tok_ref[...].astype(F32), og_ref[...].astype(F32)], axis=0).astype(BF)
    lane = lax.broadcasted_iota(I32, (TOK, 128), 1)
    row = lax.broadcasted_iota(I32, (TOK, 128), 0)
    ids, gates = ids_ref[...], gates_ref[...]
    gate = jnp.zeros((TOK, 128), F32)
    for k in range(TOP):
        gate += jnp.where(ids[:, k : k + 1] == lax.div(lane, 2), gates[:, k : k + 1], 0.0)
    used = jnp.where(gate > 0.0, 1, 0)
    rank = jnp.zeros((TOK, 128), I32)
    for t in range(TOK - 1):
        rank += jnp.where(row > t, used[t : t + 1, :], 0)
    tile = jnp.where(rank == lax.rem(lane, 2), gate, 0.0)
    table[0, 0:8] = tile
    table[0, 8:16] = tile

    pl.semaphore_wait(barrier, len(others))

    ring = {}

    def hop(s):
        for name, slots, step in (("R", R, 1), ("L", L, -1)):
            if s not in slots:
                continue
            src, dst = slots[s - 1], slots[s]
            ring[name, s] = (
                remote(table.at[src], table.at[dst], at_s.at[dst], at_r.at[dst], at_z(step)),
                remote(zbuf.at[src], zbuf.at[dst], az_s.at[dst], az_r.at[dst], at_z(step)),
            )

    def landed(s):
        for name in "RL":
            for copy in ring.get((name, s), ()):
                copy.wait_recv()

    def pick(g):
        tt[g] = table[8 * g : 8 * g + 8].reshape(128, 128).T
        block = lax.div(lane, 16)
        pieces = []
        for j in range(NY):
            for s in range(2):
                at = 2 * (z * NY + lax.rem(y + j, NY)) + s
                pieces.append(jnp.where(block == row, tt[g, pl.ds(at, 1), :], 0.0))
        weighted = jnp.concatenate(pieces, axis=0)
        second = lax.div(lax.rem(lax.broadcasted_iota(I32, (64, 128), 1), 16), 8) == 1
        hit = weighted > 0.0
        one_x = jnp.where(hit & ~second, 1.0, 0.0).astype(BF)
        one_g = jnp.where(hit & second, 1.0, 0.0).astype(BF)
        scale = jnp.sum(jnp.where(second, weighted, 0.0), axis=1, keepdims=True)
        picks[g, 0] = one_x
        picks[g, 1] = one_g
        blocks = zbuf[8 * g : 8 * g + 8].reshape(128, D)
        rows_x = jnp.dot(one_x, blocks, preferred_element_type=F32).astype(BF)
        rows_g = (jnp.dot(one_g, blocks, preferred_element_type=F32) * scale).astype(BF)
        sent = []
        for j in range(1, NY):
            bsend[g, j - 1, 0] = rows_x[16 * j : 16 * j + 16]
            bsend[g, j - 1, 1] = rows_g[16 * j : 16 * j + 16]
            sent.append(
                remote(
                    bsend.at[g, j - 1], xg.at[g, :, 0, 0, NY - j],
                    y_s.at[g, j - 1], y_r.at[g, j - 1], at_y(j),
                )
            )
        xg[g, 0, 0, 0, 0] = rows_x[0:16]
        xg[g, 1, 0, 0, 0] = rows_g[0:16]
        return sent

    def to_sibling(g, k):
        return remote(xg.at[g, :, k, 0], xg.at[g, :, k, 1], k_s.at[g, k], k_r.at[g, k], sibling)

    def spread(g, sent):
        for copy in sent:
            copy.wait_recv()
        own = xg.at[g, :, 0, 0]
        right = remote(own, xg.at[g, :, 3, 0], x_s.at[g, 0], x_r.at[g, 0], at_x(1))
        left = remote(own, xg.at[g, :, 1, 0], x_s.at[g, 1], x_r.at[g, 1], at_x(-1))
        return right, left, [to_sibling(g, 0)]

    def forward(g, state):
        right, left, kin = state
        right.wait_recv()
        a = remote(xg.at[g, 0, 3, 0], xg.at[g, 0, 2, 0], x_s.at[g, 2], x_r.at[g, 2], at_x(1))
        kin.append(to_sibling(g, 3))
        left.wait_recv()
        b = remote(xg.at[g, 1, 1, 0], xg.at[g, 1, 2, 0], x_s.at[g, 3], x_r.at[g, 3], at_x(-1))
        kin.append(to_sibling(g, 1))
        return a, b, kin

    def last(g, state):
        a, b, kin = state
        a.wait_recv()
        b.wait_recv()
        kin.append(to_sibling(g, 2))
        return kin

    rows = NX * 2 * NY * 16

    def compute(g, kin):
        for copy in kin:
            copy.wait_recv()
        pre = jnp.dot(xg[g, 0].reshape(rows, D), wp[...], preferred_element_type=F32)
        act_grad = contract_last(xg[g, 1].reshape(rows, D), wd[...])
        gate_pre, up_pre = pre[:, :HID], pre[:, HID:]
        sig = jax.nn.sigmoid(gate_pre)
        silu = gate_pre * sig
        act[g] = (silu * up_pre).astype(BF)
        pg[g, :, HID:] = (act_grad * silu).astype(BF)
        pg[g, :, :HID] = (act_grad * up_pre * sig * (1.0 + gate_pre * (1.0 - sig))).astype(BF)

        @pl.loop(0, D // 512)
        def _(n):
            cols = pl.ds(pl.multiple_of(n * 512, 512), 512)
            out = contract_last(pg[g], wp[cols, :]).astype(BF)
            term[g, :, :, :, :, cols] = out.reshape(NX, 2, NY, 16, 512)

        return {
            k: remote(term.at[g, k, 1], cbuf.at[g, k], c_s.at[g, k], c_r.at[g, k], sibling)
            for k in (2, 1, 3, 0)
        }

    def weight_grads(g):
        @pl.loop(0, D // 256)
        def _(m):
            cols = pl.ds(pl.multiple_of(m * 256, 256), 256)
            pair = contract_first(xg[g, 0, :, :, :, :, cols].reshape(rows, 256), pg[g])
            down = contract_first(act[g], xg[g, 1, :, :, :, :, cols].reshape(rows, 256))
            if g == 0:
                gg_ref[cols, :] = pair[:, :HID]
                gu_ref[cols, :] = pair[:, HID:]
                gd_ref[:, cols] = down
            else:
                gg_ref[cols, :] += pair[:, :HID]
                gu_ref[cols, :] += pair[:, HID:]
                gd_ref[:, cols] += down

    def summed(g, k, part_of=slice(0, NY)):
        return term[g, k, 0, part_of].astype(F32) + cbuf[g, k, part_of].astype(F32)

    lo, hi = slice(0, 2), slice(2, 4)

    def back_first(g, twins):
        twins[2].wait_recv()
        pbuf[g, 1] = summed(g, 2).astype(BF)
        d_right = remote(pbuf.at[g, 1, 0:2], dbuf.at[g, 0], d_s.at[g, 0], d_r.at[g, 0], at_x(1))
        d_left = remote(pbuf.at[g, 1, 2:4], dbuf.at[g, 1], d_s.at[g, 1], d_r.at[g, 1], at_x(-1))
        twins[1].wait_recv()
        pbuf[g, 0, hi] = summed(g, 1, hi).astype(BF)
        e0 = remote(pbuf.at[g, 0, 2:4], ebuf.at[g, 0, 2:4], e_s.at[g, 0], e_r.at[g, 0], at_x(1))
        twins[3].wait_recv()
        pbuf[g, 2, lo] = summed(g, 3, lo).astype(BF)
        e1 = remote(pbuf.at[g, 2, 0:2], ebuf.at[g, 1, 0:2], e_s.at[g, 1], e_r.at[g, 1], at_x(-1))
        return d_right, d_left, e0, e1, twins[0]

    def back_second(g, state):
        d_right, d_left, e0, e1, twin = state
        d_right.wait_recv()
        pbuf[g, 0, lo] = (summed(g, 1, lo) + dbuf[g, 0].astype(F32)).astype(BF)
        e2 = remote(pbuf.at[g, 0, 0:2], ebuf.at[g, 0, 0:2], e_s.at[g, 2], e_r.at[g, 2], at_x(1))
        d_left.wait_recv()
        pbuf[g, 2, hi] = (summed(g, 3, hi) + dbuf[g, 1].astype(F32)).astype(BF)
        e3 = remote(pbuf.at[g, 2, 2:4], ebuf.at[g, 1, 2:4], e_s.at[g, 3], e_r.at[g, 3], at_x(-1))
        return e0, e1, e2, e3, twin

    def back_y(g, state):
        for copy in state:
            copy.wait_recv()
        total = (summed(g, 0) + ebuf[g, 0].astype(F32) + ebuf[g, 1].astype(F32)).astype(BF)
        fbuf[g] = total[1:NY]
        rbuf[g, 0] = total[0]
        return [
            remote(fbuf.at[g, k - 1], rbuf.at[g, NY - k], f_s.at[g, k - 1], f_r.at[g, k - 1], at_y(k))
            for k in range(1, NY)
        ]

    def combine(g, sent):
        for copy in sent:
            copy.wait_recv()
        back = rbuf[g].reshape(64, D)
        out = contract_first(picks[g, 0], back[:, :HALF]) + contract_first(picks[g, 1], back[:, HALF:])
        return out.reshape(8, 16, HALF)

    hop(1)
    for s in range(1, 4):
        landed(s)
        hop(s + 1)
    ring["R", 4][0].wait_recv()
    ring["R", 4][1].wait_recv()
    later = [ring.pop(("L", 4))]
    ring.pop(("R", 4))
    dst = R[5]
    ring["R", 5] = (
        remote(table.at[R[4]], table.at[dst], at_s.at[dst], at_r.at[dst], at_z(1)),
        remote(zbuf.at[R[4]], zbuf.at[dst], az_s.at[dst], az_r.at[dst], at_z(1)),
    )
    for copy in later[0]:
        copy.wait_recv()
    dst = L[5]
    ring["L", 5] = (
        remote(table.at[L[4]], table.at[dst], at_s.at[dst], at_r.at[dst], at_z(-1)),
        remote(zbuf.at[L[4]], zbuf.at[dst], az_s.at[dst], az_r.at[dst], at_z(-1)),
    )
    sent0 = pick(0)
    landed(5)
    hop(6)
    near = spread(0, sent0)
    for s in (6, 7):
        landed(s)
        hop(s + 1)
    landed(8)
    sent1 = pick(1)
    far = spread(1, sent1)
    near = forward(0, near)
    near = last(0, near)
    far = forward(1, far)
    for load in loads:
        load.wait()
    twins0 = compute(0, near)
    far = last(1, far)
    back0 = back_first(0, twins0)
    twins1 = compute(1, far)
    back0 = back_second(0, back0)
    back1 = back_first(1, twins1)
    y0 = back_y(0, back0)
    weight_grads(0)
    back1 = back_second(1, back1)
    s0 = combine(0, y0)
    part[...] = s0
    sbuf[0:7] = s0[1:8].astype(BF)
    into = []
    for k in range(1, 8):
        to = -k if k <= 4 else k - 4
        into.append(remote(sbuf.at[k - 1], nbuf.at[k - 1], n_s.at[k - 1], n_r.at[k - 1], at_z(to)))
    weight_grads(1)
    y1 = back_y(1, back1)
    s1 = combine(1, y1)
    chain = [None, None]
    for step in range(4):
        for side, base, toward, home in ((0, 3, -1, -5), (1, 7, 1, 4)):
            value = s1[base - step]
            if step > 0:
                chain[side].wait_recv()
                value = value + hbuf[side, step - 1].astype(F32)
            at = 7 + 4 * side + step
            sbuf[at] = value.astype(BF)
            if step < 3:
                chain[side] = remote(
                    sbuf.at[at], hbuf.at[side, step], h_s.at[side, step], h_r.at[side, step], at_z(toward)
                )
            else:
                into.append(remote(sbuf.at[at], nbuf.at[7 + side], n_s.at[7 + side], n_r.at[7 + side], at_z(home)))
    total = part[0]
    for k, copy in enumerate(into):
        copy.wait_recv()
        total = total + nbuf[k].astype(F32)
    gtok_ref[:, :HALF] = total[0:8].astype(BF)
    gtok_ref[:, HALF:] = total[8:16].astype(BF)
    for copy in started:
        copy.wait_send()


def shards(tokens, out_grad, ids, gates, w_gate, w_up, w_down):
    vmem = pl.BlockSpec(memory_space=pltpu.VMEM)
    hbm = pl.BlockSpec(memory_space=pl.ANY)
    dma = pltpu.SemaphoreType.DMA
    pair = [dma((2, 3)), dma((2, 3))]
    four = [dma((2, 4)), dma((2, 4))]
    gtok, gg, gu, gd = pl.pallas_call(
        kernel,
        out_shape=(
            jax.ShapeDtypeStruct((TOK, D), BF),
            jax.ShapeDtypeStruct((D, HID), F32),
            jax.ShapeDtypeStruct((D, HID), F32),
            jax.ShapeDtypeStruct((HID, D), F32),
        ),
        in_specs=[vmem] * 4 + [hbm] * 3,
        out_specs=(vmem,) * 4,
        scratch_shapes=[
            pltpu.VMEM((NZ, 16, 128), F32),
            pltpu.VMEM((2, 128, 128), F32),
            pltpu.VMEM((NZ, 16, D), BF),
            pltpu.VMEM((2, 2, 64, 128), BF),
            pltpu.VMEM((2, 3, 2, 16, D), BF),
            pltpu.VMEM((2, 2, NX, 2, NY, 16, D), BF),
            pltpu.VMEM((D, 2 * HID), BF),
            pltpu.VMEM((HID, D), BF),
            pltpu.VMEM((2, 512, 2 * HID), BF),
            pltpu.VMEM((2, 512, HID), BF),
            pltpu.VMEM((2, NX, 2, NY, 16, D), BF),
            pltpu.VMEM((2, NX, NY, 16, D), BF),
            pltpu.VMEM((2, 3, NY, 16, D), BF),
            pltpu.VMEM((2, 2, 2, 16, D), BF),
            pltpu.VMEM((2, 2, NY, 16, D), BF),
            pltpu.VMEM((2, 3, 16, D), BF),
            pltpu.VMEM((2, NY, 16, D), BF),
            pltpu.VMEM((8, 16, HALF), F32),
            pltpu.VMEM((15, 16, HALF), BF),
            pltpu.VMEM((9, 16, HALF), BF),
            pltpu.VMEM((2, 3, 16, HALF), BF),
            dma((3,)),
            dma((NZ,)), dma((NZ,)), dma((NZ,)), dma((NZ,)),
            *pair, *four, *four, *four,
            dma((2, 2)), dma((2, 2)), *four, *pair,
            dma((9,)), dma((9,)), *pair,
        ],
        compiler_params=pltpu.CompilerParams(
            collective_id=0, has_side_effects=True, vmem_limit_bytes=52 * 2**20
        ),
    )(ids, gates, tokens, out_grad, w_gate[0], w_up[0], w_down[0])
    return gtok, gg[None], gu[None], gd[None]


def solution(mesh):
    tok = P(("dp", "expert"), None)
    col, row = P("expert", None, "dp"), P("expert", "dp", None)
    return jax.shard_map(
        shards,
        mesh=mesh,
        in_specs=(tok, tok, tok, tok, col, col, row),
        out_specs=(tok, col, col, row),
        check_vma=False,
    )
```

```python
import jax
import jax.numpy as jnp
from jax import lax
from jax.experimental import pallas as pl
from jax.experimental.pallas import tpu as pltpu
from jax.sharding import PartitionSpec as P

BF, F32, I32 = jnp.bfloat16, jnp.float32, jnp.int32
NX, NY, NZ = 4, 4, 16
TOK, TOP, D, HID = 8, 8, 2048, 128
HALF = D // 2
R = {0: 0, 1: 1, 2: 3, 3: 5, 4: 7, 5: 9, 6: 11, 7: 13, 8: 15}
L = {0: 0, 1: 2, 2: 4, 3: 6, 4: 8, 5: 10, 6: 12, 7: 14}


def contract_last(a, b):
    return lax.dot_general(a, b, (((1,), (1,)), ((), ())), preferred_element_type=F32)


def contract_first(a, b):
    return lax.dot_general(a, b, (((0,), (0,)), ((), ())), preferred_element_type=F32)


def kernel(
    ids_hbm, gates_hbm, both_ref, wg_hbm, wu_hbm, wd_hbm,
    gtok_ref, gg_ref, gu_ref, gd_ref,
    ids_ref, gates_ref, table, tt, zbuf, weights, bsend, ybuf, xg, wp, wd, pg, act, term, cbuf, pbuf, dbuf, ebuf,
    fbuf, rbuf, part, sbuf, nbuf, hbuf,
    wsem, az_s, az_r, at_s, at_r, y_s, y_r, x_s, x_r, k_s, k_r, c_s, c_r,
    d_s, d_r, e_s, e_r, f_s, f_r, n_s, n_r, h_s, h_r,
):
    dp, ex = lax.axis_index("dp"), lax.axis_index("expert")
    x, c = lax.div(dp, 2), lax.rem(dp, 2)
    z, y = lax.div(ex, NY), lax.rem(ex, NY)

    def at_z(k):
        return (dp, lax.rem(z + k + NZ, NZ) * NY + y)

    def at_y(k):
        return (dp, z * NY + lax.rem(y + k, NY))

    def at_x(k):
        return (lax.rem(x + k + NX, NX) * 2 + c, ex)

    sibling = (x * 2 + 1 - c, ex)
    started = []

    def remote(src, dst, ss, rs, device):
        copy = pltpu.make_async_remote_copy(
            src_ref=src, dst_ref=dst, send_sem=ss, recv_sem=rs,
            device_id=device, device_id_type=pl.DeviceIdType.MESH,
        )
        copy.start()
        started.append(copy)
        return copy

    barrier = pltpu.get_barrier_semaphore()
    others = [at_z(k) for k in (1, 2, 3, 4, 5, -1, -2, -3, -4, -5)]
    others += [at_y(k) for k in (1, 2, 3)] + [at_x(1), at_x(-1), sibling]
    for device in others:
        pl.semaphore_signal(barrier, inc=1, device_id=device, device_id_type=pl.DeviceIdType.MESH)

    loads = [
        pltpu.make_async_copy(wg_hbm, wp.at[:, 0:HID], wsem.at[0]),
        pltpu.make_async_copy(wu_hbm, wp.at[:, HID : 2 * HID], wsem.at[1]),
        pltpu.make_async_copy(wd_hbm, wd, wsem.at[2]),
    ]
    small = [
        pltpu.make_async_copy(ids_hbm, ids_ref, wsem.at[3]),
        pltpu.make_async_copy(gates_hbm, gates_ref, wsem.at[4]),
    ]
    for load in small + loads:
        load.start()

    zbuf[0] = both_ref[...]
    for load in small:
        load.wait()
    lane = lax.broadcasted_iota(I32, (TOK, 128), 1)
    row = lax.broadcasted_iota(I32, (TOK, 128), 0)
    ids, gates = ids_ref[...], gates_ref[...]
    gate = jnp.zeros((TOK, 128), F32)
    for k in range(TOP):
        gate += jnp.where(ids[:, k : k + 1] == lax.div(lane, 2), gates[:, k : k + 1], 0.0)
    used = jnp.where(gate > 0.0, 1, 0)
    rank = jnp.zeros((TOK, 128), I32)
    for t in range(TOK - 1):
        rank += jnp.where(row > t, used[t : t + 1, :], 0)
    tile = jnp.where(rank == lax.rem(lane, 2), gate, 0.0)
    table[0, 0:8] = tile
    table[0, 8:16] = tile

    pl.semaphore_wait(barrier, len(others))

    ring = {}

    def hop(s):
        for name, slots, step in (("R", R, 1), ("L", L, -1)):
            if s not in slots:
                continue
            src, dst = slots[s - 1], slots[s]
            ring[name, s] = (
                remote(table.at[src], table.at[dst], at_s.at[dst], at_r.at[dst], at_z(step)),
                remote(zbuf.at[src], zbuf.at[dst], az_s.at[dst], az_r.at[dst], at_z(step)),
            )

    def landed(s):
        for name in "RL":
            for copy in ring.get((name, s), ()):
                copy.wait_recv()

    def pick(q):
        wide = jnp.concatenate([table[4 * q : 4 * q + 4].reshape(64, 128), jnp.zeros((64, 128), F32)], axis=0)
        tt[q] = wide.T
        place = lax.broadcasted_iota(I32, (8, 64), 0)
        block = lax.div(lax.broadcasted_iota(I32, (8, 64), 1), 16)
        pieces = []
        for j in range(NY):
            at = 2 * (z * NY + lax.rem(y + j, NY))
            slot = [tt[q, pl.ds(at + s, 1), 0:64] for s in range(2)]
            pieces.append(jnp.where(block == lax.rem(place, 4), jnp.where(place < 4, slot[0], slot[1]), 0.0))
        weighted = jnp.concatenate(pieces, axis=0)
        weights[q] = weighted
        second = lax.rem(lax.div(lax.broadcasted_iota(I32, (32, 64), 1), 8), 2) == 1
        hit = weighted > 0.0
        one_x = jnp.where(hit & ~second, 1.0, 0.0).astype(BF)
        one_g = jnp.where(hit & second, 1.0, 0.0).astype(BF)
        scale = jnp.sum(jnp.where(second, weighted, 0.0), axis=1, keepdims=True)
        blocks = zbuf[4 * q : 4 * q + 4].reshape(64, D)
        rows_x = jnp.dot(one_x, blocks, preferred_element_type=F32)
        rows_g = jnp.dot(one_g, blocks, preferred_element_type=F32) * scale
        sent = []
        for j in range(NY):
            cut = slice(8 * j, 8 * j + 8)
            tile = jnp.concatenate([rows_x[cut], rows_g[cut]], axis=0).astype(BF)
            if j == 0:
                ybuf[q, 0] = tile
                continue
            bsend[q, j - 1] = tile
            sent.append(
                remote(
                    bsend.at[q, j - 1], ybuf.at[q, NY - j],
                    y_s.at[q, j - 1], y_r.at[q, j - 1], at_y(j),
                )
            )
        return sent

    def held(q, *at):
        g, h = divmod(q, 2)
        return xg.at[(g, *at[:3], h)] if len(at) > 2 else xg.at[g, :, at[0], at[1], h]

    def to_sibling(q, k):
        return remote(held(q, k, 0), held(q, k, 1), k_s.at[q, k], k_r.at[q, k], sibling)

    def spread(q, sent):
        for copy in sent:
            copy.wait_recv()
        g, h = divmod(q, 2)
        tiles = [ybuf[q, j].astype(F32) for j in range(NY)]
        xg[g, 0, 0, 0, h] = jnp.concatenate([t[0:8] for t in tiles], axis=0).astype(BF)
        xg[g, 1, 0, 0, h] = jnp.concatenate([t[8:16] for t in tiles], axis=0).astype(BF)
        right = remote(held(q, 0, 0), held(q, 3, 0), x_s.at[q, 0], x_r.at[q, 0], at_x(1))
        left = remote(held(q, 0, 0), held(q, 1, 0), x_s.at[q, 1], x_r.at[q, 1], at_x(-1))
        return right, left, [to_sibling(q, 0)]

    def forward(q, state):
        right, left, kin = state
        right.wait_recv()
        a = remote(held(q, 0, 3, 0), held(q, 0, 2, 0), x_s.at[q, 2], x_r.at[q, 2], at_x(1))
        left.wait_recv()
        b = remote(held(q, 1, 1, 0), held(q, 1, 2, 0), x_s.at[q, 3], x_r.at[q, 3], at_x(-1))
        kin.append(to_sibling(q, 3))
        kin.append(to_sibling(q, 1))
        return a, b, kin

    def last(q, state):
        a, b, kin = state
        a.wait_recv()
        b.wait_recv()
        kin.append(to_sibling(q, 2))
        return kin

    rows = NX * 2 * 64

    def compute(g):
        pre = jnp.dot(xg[g, 0].reshape(rows, D), wp[...], preferred_element_type=F32)
        act_grad = contract_last(xg[g, 1].reshape(rows, D), wd[...])
        gate_pre, up_pre = pre[:, :HID], pre[:, HID:]
        sig = jax.nn.sigmoid(gate_pre)
        silu = gate_pre * sig
        act[g] = (silu * up_pre).astype(BF)
        pg[g, :, HID:] = (act_grad * silu).astype(BF)
        pg[g, :, :HID] = (act_grad * up_pre * sig * (1.0 + gate_pre * (1.0 - sig))).astype(BF)

        @pl.loop(0, D // 512)
        def _(n):
            cols = pl.ds(pl.multiple_of(n * 512, 512), 512)
            out = contract_last(pg[g], wp[cols, :]).astype(BF)
            term[g, :, :, :, :, cols] = out.reshape(NX, 2, 2, 32, 512)

        return {
            k: remote(term.at[g, k, 1], cbuf.at[g, k], c_s.at[g, k], c_r.at[g, k], sibling)
            for k in (2, 1, 3, 0)
        }

    def weight_grads(g):
        @pl.loop(0, D // 256)
        def _(m):
            cols = pl.ds(pl.multiple_of(m * 256, 256), 256)
            pair = contract_first(xg[g, 0, :, :, :, :, cols].reshape(rows, 256), pg[g])
            down = contract_first(act[g], xg[g, 1, :, :, :, :, cols].reshape(rows, 256))
            if g == 0:
                gg_ref[cols, :] = pair[:, :HID]
                gu_ref[cols, :] = pair[:, HID:]
                gd_ref[:, cols] = down
            else:
                gg_ref[cols, :] += pair[:, :HID]
                gu_ref[cols, :] += pair[:, HID:]
                gd_ref[:, cols] += down

    def summed(g, k, part_of=slice(0, 2)):
        return term[g, k, 0, part_of].astype(F32) + cbuf[g, k, part_of].astype(F32)

    lo, hi = 0, 1

    def back_first(g, twins):
        twins[2].wait_recv()
        pbuf[g, 1] = summed(g, 2).astype(BF)
        d_right = remote(pbuf.at[g, 1, 0], dbuf.at[g, 0], d_s.at[g, 0], d_r.at[g, 0], at_x(1))
        d_left = remote(pbuf.at[g, 1, 1], dbuf.at[g, 1], d_s.at[g, 1], d_r.at[g, 1], at_x(-1))
        twins[1].wait_recv()
        pbuf[g, 0, hi] = summed(g, 1, hi).astype(BF)
        e0 = remote(pbuf.at[g, 0, 1], ebuf.at[g, 0, 1], e_s.at[g, 0], e_r.at[g, 0], at_x(1))
        twins[3].wait_recv()
        pbuf[g, 2, lo] = summed(g, 3, lo).astype(BF)
        e1 = remote(pbuf.at[g, 2, 0], ebuf.at[g, 1, 0], e_s.at[g, 1], e_r.at[g, 1], at_x(-1))
        return d_right, d_left, e0, e1, twins[0]

    def back_second(g, state):
        d_right, d_left, e0, e1, twin = state
        d_right.wait_recv()
        pbuf[g, 0, lo] = (summed(g, 1, lo) + dbuf[g, 0].astype(F32)).astype(BF)
        e2 = remote(pbuf.at[g, 0, 0], ebuf.at[g, 0, 0], e_s.at[g, 2], e_r.at[g, 2], at_x(1))
        d_left.wait_recv()
        pbuf[g, 2, hi] = (summed(g, 3, hi) + dbuf[g, 1].astype(F32)).astype(BF)
        e3 = remote(pbuf.at[g, 2, 1], ebuf.at[g, 1, 1], e_s.at[g, 3], e_r.at[g, 3], at_x(-1))
        return e0, e1, e2, e3, twin

    def back_y(g, state):
        for copy in state:
            copy.wait_recv()
        total = summed(g, 0) + ebuf[g, 0].astype(F32) + ebuf[g, 1].astype(F32)
        for k in range(NY):
            cut = slice(8 * k, 8 * k + 8)
            tile = jnp.concatenate([total[0, cut], total[1, cut]], axis=0).astype(BF)
            if k == 0:
                rbuf[g, 0] = tile
            else:
                fbuf[g, k - 1] = tile
        return [
            remote(fbuf.at[g, k - 1], rbuf.at[g, NY - k], f_s.at[g, k - 1], f_r.at[g, k - 1], at_y(k))
            for k in range(1, NY)
        ]

    def combine(g, sent):
        for copy in sent:
            copy.wait_recv()
        back = rbuf[g].reshape(64, D)
        second = lax.rem(lax.div(lax.broadcasted_iota(I32, (64, 64), 1), 8), 2) == 1
        none = jnp.zeros((8, 64), F32)
        made = []
        for h in range(2):
            weighted = weights[2 * g + h]
            pieces = []
            for j in range(NY):
                piece = weighted[8 * j : 8 * j + 8]
                pieces += [piece, none] if h == 0 else [none, piece]
            hit = jnp.concatenate(pieces, axis=0) > 0.0
            one_lo = jnp.where(hit & ~second, 1.0, 0.0).astype(BF)
            one_hi = jnp.where(hit & second, 1.0, 0.0).astype(BF)
            made.append(contract_first(one_lo, back[:, :HALF]) + contract_first(one_hi, back[:, HALF:]))
        return jnp.concatenate(made, axis=0).reshape(8, 16, HALF)

    scope = jax.named_scope
    with scope("hop2"):
        hop(1)
        landed(1)
        hop(2)
        landed(2)
        hop(3)
    with scope("pick0"):
        sent0 = pick(0)
    with scope("hop3"):
        landed(3)
        hop(4)
    with scope("spread0"):
        q0 = spread(0, sent0)
    with scope("hop4"):
        landed(4)
        hop(5)
    with scope("pick1"):
        sent1 = pick(1)
    with scope("hop5"):
        landed(5)
        hop(6)
    with scope("spread1"):
        q1 = spread(1, sent1)
    with scope("hop6"):
        landed(6)
        hop(7)
    with scope("pick2"):
        sent2 = pick(2)
    with scope("forward0"):
        q0 = forward(0, q0)
    with scope("hop7"):
        landed(7)
        hop(8)
    with scope("spread2"):
        q2 = spread(2, sent2)
    with scope("hop8"):
        landed(8)
    with scope("pick3"):
        sent3 = pick(3)
    with scope("forward1"):
        q1 = forward(1, q1)
    with scope("spread3"):
        q3 = spread(3, sent3)
    with scope("last01"):
        near = last(0, q0)
        near += last(1, q1)
    with scope("forward2"):
        q2 = forward(2, q2)
    for load in loads:
        load.wait()
    with scope("kin_near"):
        for copy in near:
            copy.wait_recv()
    with scope("compute_near"):
        twins0 = compute(0)
    with scope("forward3"):
        q3 = forward(3, q3)
    with scope("last2"):
        far = last(2, q2)
    with scope("back_first_near"):
        back0 = back_first(0, twins0)
    with scope("last3"):
        far += last(3, q3)
    with scope("kin_far"):
        for copy in far:
            copy.wait_recv()
    with scope("compute_far"):
        twins1 = compute(1)
    with scope("back_second_near"):
        back0 = back_second(0, back0)
    with scope("back_first_far"):
        back1 = back_first(1, twins1)
    with scope("back_y_near"):
        y0 = back_y(0, back0)
    with scope("grads_near"):
        weight_grads(0)
    with scope("back_second_far"):
        back1 = back_second(1, back1)
    with scope("combine_near"):
        s0 = combine(0, y0)
        part[...] = s0
        sbuf[0:7] = s0[1:8].astype(BF)
        into = []
        for k in range(1, 8):
            to = -(k + 1) // 2 if k % 2 else k // 2
            into.append(remote(sbuf.at[k - 1], nbuf.at[k - 1], n_s.at[k - 1], n_r.at[k - 1], at_z(to)))
    with scope("grads_far"):
        weight_grads(1)
    with scope("back_y_far"):
        y1 = back_y(1, back1)
    with scope("combine_far"):
        s1 = combine(1, y1)
    chain = [None, None]
    with scope("chain"):
        for step in range(4):
            for side, base, toward, home in ((0, R[8], -1, -5), (1, L[7], 1, 4)):
                value = s1[base - 8 - 2 * step]
                if step > 0:
                    chain[side].wait_recv()
                    value = value + hbuf[side, step - 1].astype(F32)
                at = 7 + 4 * side + step
                sbuf[at] = value.astype(BF)
                if step < 3:
                    chain[side] = remote(
                        sbuf.at[at], hbuf.at[side, step], h_s.at[side, step], h_r.at[side, step], at_z(toward)
                    )
                else:
                    into.append(remote(sbuf.at[at], nbuf.at[7 + side], n_s.at[7 + side], n_r.at[7 + side], at_z(home)))
    with scope("finish"):
        total = part[0]
        for k, copy in enumerate(into):
            copy.wait_recv()
            total = total + nbuf[k].astype(F32)
        gtok_ref[:, :HALF] = total[0:8].astype(BF)
        gtok_ref[:, HALF:] = total[8:16].astype(BF)
        for copy in started:
            copy.wait_send()


def write_out(a_ref, b_ref, c_ref, a_out, b_out, c_out, sem):
    pairs = ((a_ref, a_out), (b_ref, b_out), (c_ref, c_out))
    copies = [pltpu.make_async_copy(i, o, sem.at[k]) for k, (i, o) in enumerate(pairs)]
    for copy in copies:
        copy.start()
    for copy in copies:
        copy.wait()


def shards(tokens, out_grad, ids, gates, w_gate, w_up, w_down):
    vmem = pl.BlockSpec(memory_space=pltpu.VMEM)
    hbm = pl.BlockSpec(memory_space=pltpu.HBM)
    dma = pltpu.SemaphoreType.DMA
    pair = [dma((2, 3)), dma((2, 3))]
    four = [dma((2, 4)), dma((2, 4))]
    both = jnp.concatenate([tokens, out_grad], axis=0)
    made = pl.pallas_call(
        kernel,
        out_shape=(
            jax.ShapeDtypeStruct((TOK, D), BF),
            pltpu.VMEM((D, HID), F32),
            pltpu.VMEM((D, HID), F32),
            pltpu.VMEM((HID, D), F32),
        ),
        in_specs=[hbm] * 2 + [vmem] + [hbm] * 3,
        out_specs=(vmem,) * 4,
        scratch_shapes=[
            pltpu.VMEM((TOK, TOP), I32),
            pltpu.VMEM((TOK, TOP), F32),
            pltpu.VMEM((NZ, 16, 128), F32),
            pltpu.VMEM((4, 128, 128), F32),
            pltpu.VMEM((NZ, 16, D), BF),
            pltpu.VMEM((4, 32, 64), F32),
            pltpu.VMEM((4, 3, 16, D), BF),
            pltpu.VMEM((4, NY, 16, D), BF),
            pltpu.VMEM((2, 2, NX, 2, 2, 32, D), BF),
            pltpu.VMEM((D, 2 * HID), BF),
            pltpu.VMEM((HID, D), BF),
            pltpu.VMEM((2, 512, 2 * HID), BF),
            pltpu.VMEM((2, 512, HID), BF),
            pltpu.VMEM((2, NX, 2, 2, 32, D), BF),
            pltpu.VMEM((2, NX, 2, 32, D), BF),
            pltpu.VMEM((2, 3, 2, 32, D), BF),
            pltpu.VMEM((2, 2, 32, D), BF),
            pltpu.VMEM((2, 2, 2, 32, D), BF),
            pltpu.VMEM((2, 3, 16, D), BF),
            pltpu.VMEM((2, NY, 16, D), BF),
            pltpu.VMEM((8, 16, HALF), F32),
            pltpu.VMEM((15, 16, HALF), BF),
            pltpu.VMEM((9, 16, HALF), BF),
            pltpu.VMEM((2, 3, 16, HALF), BF),
            dma((5,)),
            dma((NZ,)), dma((NZ,)), dma((NZ,)), dma((NZ,)),
            dma((4, 3)), dma((4, 3)), dma((4, 4)), dma((4, 4)), dma((4, 4)), dma((4, 4)), *four,
            dma((2, 2)), dma((2, 2)), *four, *pair,
            dma((9,)), dma((9,)), *pair,
        ],
        compiler_params=pltpu.CompilerParams(
            collective_id=0, has_side_effects=True, vmem_limit_bytes=52 * 2**20
        ),
    )(ids, gates, both, w_gate[0], w_up[0], w_down[0])
    gg, gu, gd = pl.pallas_call(
        write_out,
        out_shape=tuple(jax.ShapeDtypeStruct(a.shape, a.dtype) for a in made[1:]),
        in_specs=[vmem] * 3,
        out_specs=(pl.BlockSpec(memory_space=pltpu.HBM),) * 3,
        scratch_shapes=[dma((3,))],
    )(*(pltpu.with_memory_space_constraint(a, pltpu.VMEM) for a in made[1:]))
    return made[0], gg[None], gu[None], gd[None]


def solution(mesh):
    tok = P(("dp", "expert"), None)
    col, row = P("expert", None, "dp"), P("expert", "dp", None)
    return jax.shard_map(
        shards,
        mesh=mesh,
        in_specs=(tok, tok, tok, tok, col, col, row),
        out_specs=(tok, col, col, row),
        check_vma=False,
    )
```

```python
import jax
import jax.numpy as jnp
from jax import lax
from jax.experimental import pallas as pl
from jax.experimental.pallas import tpu as pltpu
from jax.sharding import PartitionSpec as P

BF, F32, I32 = jnp.bfloat16, jnp.float32, jnp.int32
NX, NY, NZ = 4, 4, 16
TOK, TOP, D, HID = 8, 8, 2048, 128
HALF = D // 2
R = {0: 0, 1: 1, 2: 3, 3: 5, 4: 7, 5: 9, 6: 11, 7: 13, 8: 15}
L = {0: 0, 1: 2, 2: 4, 3: 6, 4: 8, 5: 10, 6: 12, 7: 14}


def contract_last(a, b):
    return lax.dot_general(a, b, (((1,), (1,)), ((), ())), preferred_element_type=F32)


def contract_first(a, b):
    return lax.dot_general(a, b, (((0,), (0,)), ((), ())), preferred_element_type=F32)


def kernel(
    ids_hbm, gates_hbm, both_hbm, wg_hbm, wu_hbm, wd_hbm,
    gtok_ref, gg_ref, gu_ref, gd_ref,
    ids_ref, gates_ref, table, tt, zbuf, weights, bsend, ybuf, xg, wp, wd, pg, act, term, cbuf, pbuf, dbuf, ebuf,
    fbuf, rbuf, part, sbuf, nbuf, hbuf,
    wsem, az_s, az_r, at_s, at_r, y_s, y_r, x_s, x_r, k_s, k_r, c_s, c_r,
    d_s, d_r, e_s, e_r, f_s, f_r, n_s, n_r, h_s, h_r,
):
    dp, ex = lax.axis_index("dp"), lax.axis_index("expert")
    x, c = lax.div(dp, 2), lax.rem(dp, 2)
    z, y = lax.div(ex, NY), lax.rem(ex, NY)

    def at_z(k):
        return (dp, lax.rem(z + k + NZ, NZ) * NY + y)

    def at_y(k):
        return (dp, z * NY + lax.rem(y + k, NY))

    def at_x(k):
        return (lax.rem(x + k + NX, NX) * 2 + c, ex)

    sibling = (x * 2 + 1 - c, ex)
    started = []

    def remote(src, dst, ss, rs, device):
        copy = pltpu.make_async_remote_copy(
            src_ref=src, dst_ref=dst, send_sem=ss, recv_sem=rs,
            device_id=device, device_id_type=pl.DeviceIdType.MESH,
        )
        copy.start()
        started.append(copy)
        return copy

    loads = [
        pltpu.make_async_copy(wg_hbm, wp.at[:, 0:HID], wsem.at[0]),
        pltpu.make_async_copy(wu_hbm, wp.at[:, HID : 2 * HID], wsem.at[1]),
        pltpu.make_async_copy(wd_hbm, wd, wsem.at[2]),
    ]
    small = [
        pltpu.make_async_copy(ids_hbm, ids_ref, wsem.at[3]),
        pltpu.make_async_copy(gates_hbm, gates_ref, wsem.at[4]),
        pltpu.make_async_copy(both_hbm, zbuf.at[0], wsem.at[5]),
    ]
    for load in small:
        load.start()

    barrier = pltpu.get_barrier_semaphore()
    others = [at_z(k) for k in (1, 2, 3, 4, 5, 6, 7, -1, -2, -3, -4, -5, -6, -7)]
    others += [at_y(k) for k in (1, 2, 3)] + [at_x(1), at_x(-1), sibling]
    for device in others:
        pl.semaphore_signal(barrier, inc=1, device_id=device, device_id_type=pl.DeviceIdType.MESH)
    for load in loads:
        load.start()

    small[2].wait()
    pl.semaphore_wait(barrier, len(others))

    ring = {}

    def hop(s, names="tz"):
        for name, slots, step in (("R", R, 1), ("L", L, -1)):
            if s not in slots:
                continue
            src, dst = slots[s - 1], slots[s]
            copies = ring.setdefault((name, s), [])
            if s == 2:
                src, step = slots[0], 2 * step
            if "z" in names:
                copies.append(remote(zbuf.at[src], zbuf.at[dst], az_s.at[dst], az_r.at[dst], at_z(step)))
            if "t" in names:
                copies.append(remote(table.at[src], table.at[dst], at_s.at[dst], at_r.at[dst], at_z(step)))

    hop(1, "z")
    hop(2, "z")
    small[0].wait()
    small[1].wait()

    lane = lax.broadcasted_iota(I32, (TOK, 128), 1)
    row = lax.broadcasted_iota(I32, (TOK, 128), 0)
    ids, gates = ids_ref[...], gates_ref[...]
    gate = jnp.zeros((TOK, 128), F32)
    for k in range(TOP):
        gate += jnp.where(ids[:, k : k + 1] == lax.div(lane, 2), gates[:, k : k + 1], 0.0)
    used = jnp.where(gate > 0.0, 1, 0)
    rank = jnp.zeros((TOK, 128), I32)
    for t in range(TOK - 1):
        rank += jnp.where(row > t, used[t : t + 1, :], 0)
    tile = jnp.where(rank == lax.rem(lane, 2), gate, 0.0)
    table[0] = tile

    hop(1, "t")
    hop(2, "t")

    def landed(s):
        for name in "RL":
            for copy in ring.get((name, s), ()):
                copy.wait_recv()

    def pick(q):
        tiles = table[4 * q : 4 * q + 4]
        twice = jnp.concatenate([tiles, tiles], axis=1).reshape(64, 128)
        wide = jnp.concatenate([twice, jnp.zeros((64, 128), F32)], axis=0)
        tt[q] = wide.T
        place = lax.broadcasted_iota(I32, (8, 64), 0)
        block = lax.div(lax.broadcasted_iota(I32, (8, 64), 1), 16)
        pieces = []
        for j in range(NY):
            at = 2 * (z * NY + lax.rem(y + j, NY))
            slot = [tt[q, pl.ds(at + s, 1), 0:64] for s in range(2)]
            pieces.append(jnp.where(block == lax.rem(place, 4), jnp.where(place < 4, slot[0], slot[1]), 0.0))
        weighted = jnp.concatenate(pieces, axis=0)
        weights[q] = weighted
        second = lax.rem(lax.div(lax.broadcasted_iota(I32, (32, 64), 1), 8), 2) == 1
        hit = weighted > 0.0
        one_x = jnp.where(hit & ~second, 1.0, 0.0).astype(BF)
        one_g = jnp.where(hit & second, 1.0, 0.0).astype(BF)
        scale = jnp.sum(jnp.where(second, weighted, 0.0), axis=1, keepdims=True)
        blocks = zbuf[4 * q : 4 * q + 4].reshape(64, D)
        rows_x = jnp.dot(one_x, blocks, preferred_element_type=F32)
        rows_g = jnp.dot(one_g, blocks, preferred_element_type=F32) * scale
        sent = []
        for j in range(NY):
            cut = slice(8 * j, 8 * j + 8)
            tile = jnp.concatenate([rows_x[cut], rows_g[cut]], axis=0).astype(BF)
            if j == 0:
                ybuf[q, 0] = tile
                continue
            bsend[q, j - 1] = tile
            sent.append(
                remote(
                    bsend.at[q, j - 1], ybuf.at[q, NY - j],
                    y_s.at[q, j - 1], y_r.at[q, j - 1], at_y(j),
                )
            )
        return sent

    def held(q, k, kin):
        return xg.at[q, :, k, kin]

    def to_sibling(q, k):
        return remote(held(q, k, 0), held(q, k, 1), k_s.at[q, k], k_r.at[q, k], sibling)

    def spread(q, sent):
        for copy in sent:
            copy.wait_recv()
        tiles = [ybuf[q, j].astype(F32) for j in range(NY)]
        xg[q, 0, 0, 0] = jnp.concatenate([t[0:8] for t in tiles], axis=0).astype(BF)
        xg[q, 1, 0, 0] = jnp.concatenate([t[8:16] for t in tiles], axis=0).astype(BF)
        right = remote(held(q, 0, 0), held(q, 3, 0), x_s.at[q, 0], x_r.at[q, 0], at_x(1))
        left = remote(held(q, 0, 0), held(q, 1, 0), x_s.at[q, 1], x_r.at[q, 1], at_x(-1))
        return right, left, [to_sibling(q, 0)]

    def forward(q, state):
        right, left, kin = state
        right.wait_recv()
        a = remote(xg.at[q, 0, 3, 0], xg.at[q, 0, 2, 0], x_s.at[q, 2], x_r.at[q, 2], at_x(1))
        left.wait_recv()
        b = remote(xg.at[q, 1, 1, 0], xg.at[q, 1, 2, 0], x_s.at[q, 3], x_r.at[q, 3], at_x(-1))
        kin.append(to_sibling(q, 3))
        kin.append(to_sibling(q, 1))
        return a, b, kin

    def last(q, state):
        a, b, kin = state
        a.wait_recv()
        b.wait_recv()
        kin.append(to_sibling(q, 2))
        return kin

    rows = NX * 2 * 32

    def compute(q, kin):
        for copy in kin:
            copy.wait_recv()
        pre = jnp.dot(xg[q, 0].reshape(rows, D), wp[...], preferred_element_type=F32)
        act_grad = contract_last(xg[q, 1].reshape(rows, D), wd[...])
        gate_pre, up_pre = pre[:, :HID], pre[:, HID:]
        sig = jax.nn.sigmoid(gate_pre)
        silu = gate_pre * sig
        act[q] = (silu * up_pre).astype(BF)
        pg[q, :, HID:] = (act_grad * silu).astype(BF)
        pg[q, :, :HID] = (act_grad * up_pre * sig * (1.0 + gate_pre * (1.0 - sig))).astype(BF)

        @pl.loop(0, D // 512)
        def _(n):
            cols = pl.ds(pl.multiple_of(n * 512, 512), 512)
            out = contract_last(pg[q], wp[cols, :]).astype(BF)
            term[q, :, :, :, cols] = out.reshape(NX, 2, 32, 512)

        return {
            k: remote(term.at[q, k, 1], cbuf.at[q, k], c_s.at[q, k], c_r.at[q, k], sibling)
            for k in (2, 1, 3, 0)
        }

    def weight_grads(g, half):
        pair = slice(2 * g, 2 * g + 2)

        @pl.loop(4 * half, 4 * half + 4)
        def _(m):
            cols = pl.ds(pl.multiple_of(m * 256, 256), 256)
            both = pg[pair].reshape(2 * rows, 2 * HID)
            wide = contract_first(xg[pair, 0, :, :, :, cols].reshape(2 * rows, 256), both)
            hidden = act[pair].reshape(2 * rows, HID)
            down = contract_first(hidden, xg[pair, 1, :, :, :, cols].reshape(2 * rows, 256))
            if g == 0:
                gg_ref[cols, :] = wide[:, :HID]
                gu_ref[cols, :] = wide[:, HID:]
                gd_ref[:, cols] = down
            else:
                gg_ref[cols, :] += wide[:, :HID]
                gu_ref[cols, :] += wide[:, HID:]
                gd_ref[:, cols] += down

    lo, hi, every = slice(0, 16), slice(16, 32), slice(0, 32)

    def summed(q, k, cut=every):
        return term[q, k, 0, cut].astype(F32) + cbuf[q, k, cut].astype(F32)

    def back_first(q, twins):
        twins[2].wait_recv()
        pbuf[q, 1] = summed(q, 2).astype(BF)
        d_right = remote(pbuf.at[q, 1, lo], dbuf.at[q, 0], d_s.at[q, 0], d_r.at[q, 0], at_x(1))
        d_left = remote(pbuf.at[q, 1, hi], dbuf.at[q, 1], d_s.at[q, 1], d_r.at[q, 1], at_x(-1))
        twins[1].wait_recv()
        pbuf[q, 0, hi] = summed(q, 1, hi).astype(BF)
        e0 = remote(pbuf.at[q, 0, hi], ebuf.at[q, 0, hi], e_s.at[q, 0], e_r.at[q, 0], at_x(1))
        twins[3].wait_recv()
        pbuf[q, 2, lo] = summed(q, 3, lo).astype(BF)
        e1 = remote(pbuf.at[q, 2, lo], ebuf.at[q, 1, lo], e_s.at[q, 1], e_r.at[q, 1], at_x(-1))
        return d_right, d_left, e0, e1, twins[0]

    def back_second(q, state):
        d_right, d_left, e0, e1, twin = state
        d_right.wait_recv()
        pbuf[q, 0, lo] = (summed(q, 1, lo) + dbuf[q, 0].astype(F32)).astype(BF)
        e2 = remote(pbuf.at[q, 0, lo], ebuf.at[q, 0, lo], e_s.at[q, 2], e_r.at[q, 2], at_x(1))
        d_left.wait_recv()
        pbuf[q, 2, hi] = (summed(q, 3, hi) + dbuf[q, 1].astype(F32)).astype(BF)
        e3 = remote(pbuf.at[q, 2, hi], ebuf.at[q, 1, hi], e_s.at[q, 3], e_r.at[q, 3], at_x(-1))
        return e0, e1, e2, e3, twin

    def back_y(q, state):
        for copy in state:
            copy.wait_recv()
        total = summed(q, 0) + ebuf[q, 0].astype(F32) + ebuf[q, 1].astype(F32)
        sent = []
        for k in range(NY):
            piece = total[8 * k : 8 * k + 8]
            tile = jnp.concatenate([piece[:, :HALF], piece[:, HALF:]], axis=0).astype(BF)
            if k == 0:
                rbuf[q, 0] = tile
                continue
            fbuf[q, k - 1] = tile
            sent.append(
                remote(fbuf.at[q, k - 1], rbuf.at[q, NY - k], f_s.at[q, k - 1], f_r.at[q, k - 1], at_y(k))
            )
        return sent

    def combine(q, sent):
        weighted = weights[q]
        second = lax.rem(lax.div(lax.broadcasted_iota(I32, (8, 64), 1), 8), 2) == 1
        pieces = []
        for j in range(NY):
            hit = weighted[8 * j : 8 * j + 8] > 0.0
            pieces += [jnp.where(hit & ~second, 1.0, 0.0), jnp.where(hit & second, 1.0, 0.0)]
        ones = jnp.concatenate(pieces, axis=0).astype(BF)
        for copy in sent:
            copy.wait_recv()
        return contract_first(ones, rbuf[q].reshape(64, HALF)).reshape(4, 16, HALF)

    into = []

    def home(k, step):
        into.append(remote(sbuf.at[k - 1], nbuf.at[len(into)], n_s.at[len(into)], n_r.at[len(into)], at_z(step)))

    def near_home(q, sent):
        made = combine(q, sent)
        first = 1 if q == 0 else 0
        if q == 0:
            part[...] = made[0]
        at = 4 * q + first
        sbuf[at - 1 : 4 * q + 3] = made[first:].astype(BF)
        for k in range(at, 4 * q + 4):
            home(k, -((k + 1) // 2) if k % 2 else k // 2)

    def pair_start(q, sent):
        made = combine(q, sent)
        at = 4 * q + 2
        sbuf[at - 1 : at + 1] = made[2:4].astype(BF)
        copies = [
            remote(sbuf.at[at], hbuf.at[q - 2, 0], h_s.at[q - 2, 0], h_r.at[q - 2, 0], at_z(-1)),
            remote(sbuf.at[at - 1], hbuf.at[q - 2, 1], h_s.at[q - 2, 1], h_r.at[q - 2, 1], at_z(1)),
        ]
        return made, copies

    def pair_home(q, state):
        made, copies = state
        for side, at in ((0, 4 * q + 1), (1, 4 * q)):
            copies[side].wait_recv()
            sbuf[at - 1] = (made[at - 4 * q] + hbuf[q - 2, side].astype(F32)).astype(BF)
            home(at, -((at + 1) // 2) if side == 0 else at // 2)

    scope = jax.named_scope
    with scope("hop2"):
        landed(2)
        hop(3)
    landed(1)
    with scope("pick0"):
        sent0 = pick(0)
    with scope("hop3"):
        landed(3)
        hop(4)
    with scope("spread0"):
        q0 = spread(0, sent0)
    with scope("hop4"):
        landed(4)
        hop(5)
    with scope("pick1"):
        sent1 = pick(1)
    with scope("hop5"):
        landed(5)
        hop(6)
    with scope("spread1"):
        q1 = spread(1, sent1)
    with scope("hop6"):
        landed(6)
        hop(7)
    with scope("pick2"):
        sent2 = pick(2)
    with scope("hop7"):
        landed(7)
        hop(8)
    with scope("forward0"):
        q0 = forward(0, q0)
    with scope("spread2"):
        q2 = spread(2, sent2)
    with scope("hop8"):
        landed(8)
    with scope("pick3"):
        sent3 = pick(3)
    with scope("forward1"):
        q1 = forward(1, q1)
    with scope("last0"):
        q0 = last(0, q0)
    with scope("loads"):
        for load in loads:
            load.wait()
    with scope("c0"):
        c0 = compute(0, q0)
    with scope("s3"):
        q3 = spread(3, sent3)
    with scope("f2"):
        q2 = forward(2, q2)
    with scope("l1"):
        q1 = last(1, q1)
    with scope("c1"):
        c1 = compute(1, q1)
    with scope("f3"):
        q3 = forward(3, q3)
    with scope("a0"):
        b0 = back_first(0, c0)
    with scope("a1"):
        b1 = back_first(1, c1)
    with scope("l2"):
        q2 = last(2, q2)
    with scope("c2"):
        c2 = compute(2, q2)
    with scope("b0"):
        b0 = back_second(0, b0)
    with scope("l3"):
        q3 = last(3, q3)
    with scope("b1"):
        b1 = back_second(1, b1)
    with scope("a2"):
        b2 = back_first(2, c2)
    with scope("c3"):
        c3 = compute(3, q3)
    with scope("y0"):
        y0 = back_y(0, b0)
    with scope("a3"):
        b3 = back_first(3, c3)
    with scope("b2"):
        b2 = back_second(2, b2)
    with scope("y1"):
        y1 = back_y(1, b1)
    with scope("h0"):
        near_home(0, y0)
    with scope("b3"):
        b3 = back_second(3, b3)
    with scope("h1"):
        near_home(1, y1)
    with scope("w00"):
        weight_grads(0, 0)
    with scope("y2"):
        y2 = back_y(2, b2)
    with scope("w01"):
        weight_grads(0, 1)
    with scope("p2"):
        p2 = pair_start(2, y2)
    with scope("y3"):
        y3 = back_y(3, b3)
    with scope("p2b"):
        pair_home(2, p2)
    with scope("p3"):
        p3 = pair_start(3, y3)
    with scope("w10"):
        weight_grads(1, 0)
    with scope("p3b"):
        pair_home(3, p3)
    with scope("w11"):
        weight_grads(1, 1)
    with scope("finish"):
        total = part[...]
        for k, copy in enumerate(into):
            copy.wait_recv()
            total = total + nbuf[k].astype(F32)
        gtok_ref[:, :HALF] = total[0:8].astype(BF)
        gtok_ref[:, HALF:] = total[8:16].astype(BF)
        for copy in started:
            copy.wait_send()


def write_out(a_ref, b_ref, c_ref, a_out, b_out, c_out, sem):
    pairs = ((a_ref, a_out), (b_ref, b_out), (c_ref, c_out))
    copies = [pltpu.make_async_copy(i, o, sem.at[k]) for k, (i, o) in enumerate(pairs)]
    for copy in copies:
        copy.start()
    for copy in copies:
        copy.wait()


def shards(tokens, out_grad, ids, gates, w_gate, w_up, w_down):
    vmem = pl.BlockSpec(memory_space=pltpu.VMEM)
    hbm = pl.BlockSpec(memory_space=pltpu.HBM)
    dma = pltpu.SemaphoreType.DMA
    three = [dma((4, 3)), dma((4, 3))]
    four = [dma((4, 4)), dma((4, 4))]
    both = jnp.concatenate([tokens, out_grad], axis=0)
    made = pl.pallas_call(
        kernel,
        out_shape=(
            jax.ShapeDtypeStruct((TOK, D), BF),
            pltpu.VMEM((D, HID), F32),
            pltpu.VMEM((D, HID), F32),
            pltpu.VMEM((HID, D), F32),
        ),
        in_specs=[hbm] * 6,
        out_specs=(vmem,) * 4,
        scratch_shapes=[
            pltpu.VMEM((TOK, TOP), I32),
            pltpu.VMEM((TOK, TOP), F32),
            pltpu.VMEM((NZ, 8, 128), F32),
            pltpu.VMEM((4, 128, 128), F32),
            pltpu.VMEM((NZ, 16, D), BF),
            pltpu.VMEM((4, 32, 64), F32),
            pltpu.VMEM((4, 3, 16, D), BF),
            pltpu.VMEM((4, NY, 16, D), BF),
            pltpu.VMEM((4, 2, NX, 2, 32, D), BF),
            pltpu.VMEM((D, 2 * HID), BF),
            pltpu.VMEM((HID, D), BF),
            pltpu.VMEM((4, 256, 2 * HID), BF),
            pltpu.VMEM((4, 256, HID), BF),
            pltpu.VMEM((4, NX, 2, 32, D), BF),
            pltpu.VMEM((4, NX, 32, D), BF),
            pltpu.VMEM((4, 3, 32, D), BF),
            pltpu.VMEM((4, 2, 16, D), BF),
            pltpu.VMEM((4, 2, 32, D), BF),
            pltpu.VMEM((4, 3, 16, HALF), BF),
            pltpu.VMEM((4, NY, 16, HALF), BF),
            pltpu.VMEM((16, HALF), F32),
            pltpu.VMEM((15, 16, HALF), BF),
            pltpu.VMEM((11, 16, HALF), BF),
            pltpu.VMEM((2, 2, 16, HALF), BF),
            dma((6,)),
            dma((NZ,)), dma((NZ,)), dma((NZ,)), dma((NZ,)),
            *three, *four, *four, *four,
            dma((4, 2)), dma((4, 2)), *four, *three,
            dma((11,)), dma((11,)), dma((2, 2)), dma((2, 2)),
        ],
        compiler_params=pltpu.CompilerParams(
            collective_id=0, has_side_effects=True, vmem_limit_bytes=52 * 2**20
        ),
    )(ids, gates, both, w_gate[0], w_up[0], w_down[0])
    gg, gu, gd = pl.pallas_call(
        write_out,
        out_shape=tuple(jax.ShapeDtypeStruct(a.shape, a.dtype) for a in made[1:]),
        in_specs=[vmem] * 3,
        out_specs=(pl.BlockSpec(memory_space=pltpu.HBM),) * 3,
        scratch_shapes=[dma((3,))],
    )(*(pltpu.with_memory_space_constraint(a, pltpu.VMEM) for a in made[1:]))
    return made[0], gg[None], gu[None], gd[None]


def solution(mesh):
    tok = P(("dp", "expert"), None)
    col, row = P("expert", None, "dp"), P("expert", "dp", None)
    return jax.shard_map(
        shards,
        mesh=mesh,
        in_specs=(tok, tok, tok, tok, col, col, row),
        out_specs=(tok, col, col, row),
        check_vma=False,
    )
```

```python
import jax
import jax.numpy as jnp
from jax import lax
from jax.experimental import pallas as pl
from jax.experimental.pallas import tpu as pltpu
from jax.sharding import PartitionSpec as P

BF, F32, I32 = jnp.bfloat16, jnp.float32, jnp.int32
NX, NY, NZ = 4, 4, 16
TOK, TOP, D, HID = 8, 8, 2048, 128
HALF = D // 2
R = {0: 0, 1: 1, 2: 3, 3: 5, 4: 7, 5: 9, 6: 11, 7: 13, 8: 15}
L = {0: 0, 1: 2, 2: 4, 3: 6, 4: 8, 5: 10, 6: 12, 7: 14}


def contract_last(a, b):
    return lax.dot_general(a, b, (((1,), (1,)), ((), ())), preferred_element_type=F32)


def contract_first(a, b):
    return lax.dot_general(a, b, (((0,), (0,)), ((), ())), preferred_element_type=F32)


def kernel(
    ids_hbm, gates_hbm, tok_ref, og_ref, wg_hbm, wu_hbm, wd_hbm,
    gtok_ref, gg_ref, gu_ref, gd_ref,
    ids_ref, gates_ref, table, tt, zbuf, weights, bsend, ybuf, xg, wp, wd, pg, act, term, cbuf, pbuf, dbuf, ebuf,
    fbuf, rbuf, part, sbuf, nbuf, hbuf,
    wsem, az_s, az_r, at_s, at_r, y_s, y_r, x_s, x_r, k_s, k_r, c_s, c_r,
    d_s, d_r, e_s, e_r, f_s, f_r, n_s, n_r, h_s, h_r,
):
    dp, ex = lax.axis_index("dp"), lax.axis_index("expert")
    x, c = lax.div(dp, 2), lax.rem(dp, 2)
    z, y = lax.div(ex, NY), lax.rem(ex, NY)

    def at_z(k):
        return (dp, lax.rem(z + k + NZ, NZ) * NY + y)

    def at_y(k):
        return (dp, z * NY + lax.rem(y + k, NY))

    def at_x(k):
        return (lax.rem(x + k + NX, NX) * 2 + c, ex)

    sibling = (x * 2 + 1 - c, ex)
    started = []

    def remote(src, dst, ss, rs, device):
        copy = pltpu.make_async_remote_copy(
            src_ref=src, dst_ref=dst, send_sem=ss, recv_sem=rs,
            device_id=device, device_id_type=pl.DeviceIdType.MESH,
        )
        copy.start()
        started.append(copy)
        return copy

    loads = [
        pltpu.make_async_copy(wg_hbm, wp.at[:, 0:HID], wsem.at[0]),
        pltpu.make_async_copy(wu_hbm, wp.at[:, HID : 2 * HID], wsem.at[1]),
        pltpu.make_async_copy(wd_hbm, wd, wsem.at[2]),
    ]
    small = [
        pltpu.make_async_copy(ids_hbm, ids_ref, wsem.at[3]),
        pltpu.make_async_copy(gates_hbm, gates_ref, wsem.at[4]),
    ]
    for load in small:
        load.start()

    barrier = pltpu.get_barrier_semaphore()
    others = [at_z(k) for k in (1, 2, 3, 4, 5, 6, 7, -1, -2, -3, -4, -5, -6, -7)]
    others += [at_y(k) for k in (1, 2, 3)] + [at_x(1), at_x(-1), sibling]
    for device in others:
        pl.semaphore_signal(barrier, inc=1, device_id=device, device_id_type=pl.DeviceIdType.MESH)
    for load in loads:
        load.start()

    zbuf[0] = jnp.concatenate([tok_ref[...].astype(F32), og_ref[...].astype(F32)], axis=0).astype(BF)
    pl.semaphore_wait(barrier, len(others))

    ring = {}

    def hop(s, names="tz"):
        for name, slots, step in (("R", R, 1), ("L", L, -1)):
            if s not in slots:
                continue
            src, dst = slots[s - 1], slots[s]
            copies = ring.setdefault((name, s), [])
            if s == 2:
                src, step = slots[0], 2 * step
            if "z" in names:
                copies.append(remote(zbuf.at[src], zbuf.at[dst], az_s.at[dst], az_r.at[dst], at_z(step)))
            if "t" in names:
                copies.append(remote(table.at[src], table.at[dst], at_s.at[dst], at_r.at[dst], at_z(step)))

    hop(1, "z")
    hop(2, "z")
    small[0].wait()
    small[1].wait()

    lane = lax.broadcasted_iota(I32, (TOK, 128), 1)
    row = lax.broadcasted_iota(I32, (TOK, 128), 0)
    ids, gates = ids_ref[...], gates_ref[...]
    gate = jnp.zeros((TOK, 128), F32)
    for k in range(TOP):
        gate += jnp.where(ids[:, k : k + 1] == lax.div(lane, 2), gates[:, k : k + 1], 0.0)
    used = jnp.where(gate > 0.0, 1, 0)
    rank = jnp.zeros((TOK, 128), I32)
    for t in range(TOK - 1):
        rank += jnp.where(row > t, used[t : t + 1, :], 0)
    tile = jnp.where(rank == lax.rem(lane, 2), gate, 0.0)
    table[0] = tile

    hop(1, "t")
    hop(2, "t")

    def landed(s):
        for name in "RL":
            for copy in ring.get((name, s), ()):
                copy.wait_recv()

    def pick(q):
        tiles = table[4 * q : 4 * q + 4]
        twice = jnp.concatenate([tiles, tiles], axis=1).reshape(64, 128)
        wide = jnp.concatenate([twice, jnp.zeros((64, 128), F32)], axis=0)
        tt[q] = wide.T
        place = lax.broadcasted_iota(I32, (8, 64), 0)
        block = lax.div(lax.broadcasted_iota(I32, (8, 64), 1), 16)
        pieces = []
        for j in range(NY):
            at = 2 * (z * NY + lax.rem(y + j, NY))
            slot = [tt[q, pl.ds(at + s, 1), 0:64] for s in range(2)]
            pieces.append(jnp.where(block == lax.rem(place, 4), jnp.where(place < 4, slot[0], slot[1]), 0.0))
        weighted = jnp.concatenate(pieces, axis=0)
        weights[q] = weighted
        second = lax.rem(lax.div(lax.broadcasted_iota(I32, (32, 64), 1), 8), 2) == 1
        hit = weighted > 0.0
        one_x = jnp.where(hit & ~second, 1.0, 0.0).astype(BF)
        one_g = jnp.where(hit & second, 1.0, 0.0).astype(BF)
        scale = jnp.sum(jnp.where(second, weighted, 0.0), axis=1, keepdims=True)
        blocks = zbuf[4 * q : 4 * q + 4].reshape(64, D)
        rows_x = jnp.dot(one_x, blocks, preferred_element_type=F32)
        rows_g = jnp.dot(one_g, blocks, preferred_element_type=F32) * scale
        sent = []
        for j in range(NY):
            cut = slice(8 * j, 8 * j + 8)
            tile = jnp.concatenate([rows_x[cut], rows_g[cut]], axis=0).astype(BF)
            if j == 0:
                ybuf[q, 0] = tile
                continue
            bsend[q, j - 1] = tile
            sent.append(
                remote(
                    bsend.at[q, j - 1], ybuf.at[q, NY - j],
                    y_s.at[q, j - 1], y_r.at[q, j - 1], at_y(j),
                )
            )
        return sent

    def held(q, k, kin):
        return xg.at[q, :, k, kin]

    def to_sibling(q, k):
        return remote(held(q, k, 0), held(q, k, 1), k_s.at[q, k], k_r.at[q, k], sibling)

    def spread(q, sent):
        for copy in sent:
            copy.wait_recv()
        tiles = [ybuf[q, j].astype(F32) for j in range(NY)]
        xg[q, 0, 0, 0] = jnp.concatenate([t[0:8] for t in tiles], axis=0).astype(BF)
        xg[q, 1, 0, 0] = jnp.concatenate([t[8:16] for t in tiles], axis=0).astype(BF)
        right = remote(held(q, 0, 0), held(q, 3, 0), x_s.at[q, 0], x_r.at[q, 0], at_x(1))
        left = remote(held(q, 0, 0), held(q, 1, 0), x_s.at[q, 1], x_r.at[q, 1], at_x(-1))
        return right, left, [to_sibling(q, 0)]

    def forward(q, state):
        right, left, kin = state
        right.wait_recv()
        a = remote(xg.at[q, 0, 3, 0], xg.at[q, 0, 2, 0], x_s.at[q, 2], x_r.at[q, 2], at_x(1))
        left.wait_recv()
        b = remote(xg.at[q, 1, 1, 0], xg.at[q, 1, 2, 0], x_s.at[q, 3], x_r.at[q, 3], at_x(-1))
        kin.append(to_sibling(q, 3))
        kin.append(to_sibling(q, 1))
        return a, b, kin

    def last(q, state):
        a, b, kin = state
        a.wait_recv()
        b.wait_recv()
        kin.append(to_sibling(q, 2))
        return kin

    rows = NX * 2 * 32

    def compute(q, kin):
        for copy in kin:
            copy.wait_recv()
        pre = jnp.dot(xg[q, 0].reshape(rows, D), wp[...], preferred_element_type=F32)
        act_grad = contract_last(xg[q, 1].reshape(rows, D), wd[...])
        gate_pre, up_pre = pre[:, :HID], pre[:, HID:]
        sig = jax.nn.sigmoid(gate_pre)
        silu = gate_pre * sig
        act[q] = (silu * up_pre).astype(BF)
        pg[q, :, HID:] = (act_grad * silu).astype(BF)
        pg[q, :, :HID] = (act_grad * up_pre * sig * (1.0 + gate_pre * (1.0 - sig))).astype(BF)

        @pl.loop(0, D // 512)
        def _(n):
            cols = pl.ds(pl.multiple_of(n * 512, 512), 512)
            out = contract_last(pg[q], wp[cols, :]).astype(BF)
            term[q, :, :, :, cols] = out.reshape(NX, 2, 32, 512)

        return {
            k: remote(term.at[q, k, 1], cbuf.at[q, k], c_s.at[q, k], c_r.at[q, k], sibling)
            for k in (2, 1, 3, 0)
        }

    def weight_grads(g, half):
        pair = slice(2 * g, 2 * g + 2)

        @pl.loop(4 * half, 4 * half + 4)
        def _(m):
            cols = pl.ds(pl.multiple_of(m * 256, 256), 256)
            both = pg[pair].reshape(2 * rows, 2 * HID)
            wide = contract_first(xg[pair, 0, :, :, :, cols].reshape(2 * rows, 256), both)
            hidden = act[pair].reshape(2 * rows, HID)
            down = contract_first(hidden, xg[pair, 1, :, :, :, cols].reshape(2 * rows, 256))
            if g == 0:
                gg_ref[cols, :] = wide[:, :HID]
                gu_ref[cols, :] = wide[:, HID:]
                gd_ref[:, cols] = down
            else:
                gg_ref[cols, :] += wide[:, :HID]
                gu_ref[cols, :] += wide[:, HID:]
                gd_ref[:, cols] += down

    lo, hi, every = slice(0, 16), slice(16, 32), slice(0, 32)

    def summed(q, k, cut=every):
        return term[q, k, 0, cut].astype(F32) + cbuf[q, k, cut].astype(F32)

    def back_first(q, twins):
        twins[2].wait_recv()
        pbuf[q, 1] = summed(q, 2).astype(BF)
        d_right = remote(pbuf.at[q, 1, lo], dbuf.at[q, 0], d_s.at[q, 0], d_r.at[q, 0], at_x(1))
        d_left = remote(pbuf.at[q, 1, hi], dbuf.at[q, 1], d_s.at[q, 1], d_r.at[q, 1], at_x(-1))
        twins[1].wait_recv()
        pbuf[q, 0, hi] = summed(q, 1, hi).astype(BF)
        e0 = remote(pbuf.at[q, 0, hi], ebuf.at[q, 0, hi], e_s.at[q, 0], e_r.at[q, 0], at_x(1))
        twins[3].wait_recv()
        pbuf[q, 2, lo] = summed(q, 3, lo).astype(BF)
        e1 = remote(pbuf.at[q, 2, lo], ebuf.at[q, 1, lo], e_s.at[q, 1], e_r.at[q, 1], at_x(-1))
        return d_right, d_left, e0, e1, twins[0]

    def back_second(q, state):
        d_right, d_left, e0, e1, twin = state
        d_right.wait_recv()
        pbuf[q, 0, lo] = (summed(q, 1, lo) + dbuf[q, 0].astype(F32)).astype(BF)
        e2 = remote(pbuf.at[q, 0, lo], ebuf.at[q, 0, lo], e_s.at[q, 2], e_r.at[q, 2], at_x(1))
        d_left.wait_recv()
        pbuf[q, 2, hi] = (summed(q, 3, hi) + dbuf[q, 1].astype(F32)).astype(BF)
        e3 = remote(pbuf.at[q, 2, hi], ebuf.at[q, 1, hi], e_s.at[q, 3], e_r.at[q, 3], at_x(-1))
        return e0, e1, e2, e3, twin

    def back_y(q, state):
        for copy in state:
            copy.wait_recv()
        total = summed(q, 0) + ebuf[q, 0].astype(F32) + ebuf[q, 1].astype(F32)
        sent = []
        for k in range(NY):
            piece = total[8 * k : 8 * k + 8]
            tile = jnp.concatenate([piece[:, :HALF], piece[:, HALF:]], axis=0).astype(BF)
            if k == 0:
                rbuf[q, 0] = tile
                continue
            fbuf[q, k - 1] = tile
            sent.append(
                remote(fbuf.at[q, k - 1], rbuf.at[q, NY - k], f_s.at[q, k - 1], f_r.at[q, k - 1], at_y(k))
            )
        return sent

    def combine(q, sent):
        weighted = weights[q]
        second = lax.rem(lax.div(lax.broadcasted_iota(I32, (8, 64), 1), 8), 2) == 1
        pieces = []
        for j in range(NY):
            hit = weighted[8 * j : 8 * j + 8] > 0.0
            pieces += [jnp.where(hit & ~second, 1.0, 0.0), jnp.where(hit & second, 1.0, 0.0)]
        ones = jnp.concatenate(pieces, axis=0).astype(BF)
        for copy in sent:
            copy.wait_recv()
        return contract_first(ones, rbuf[q].reshape(64, HALF)).reshape(4, 16, HALF)

    into = []

    def home(k, step):
        into.append(remote(sbuf.at[k - 1], nbuf.at[len(into)], n_s.at[len(into)], n_r.at[len(into)], at_z(step)))

    def near_home(q, sent):
        made = combine(q, sent)
        first = 1 if q == 0 else 0
        if q == 0:
            part[...] = made[0]
        at = 4 * q + first
        sbuf[at - 1 : 4 * q + 3] = made[first:].astype(BF)
        for k in range(at, 4 * q + 4):
            home(k, -((k + 1) // 2) if k % 2 else k // 2)

    def pair_start(q, sent):
        made = combine(q, sent)
        at = 4 * q + 2
        sbuf[at - 1 : at + 1] = made[2:4].astype(BF)
        copies = [
            remote(sbuf.at[at], hbuf.at[q - 2, 0], h_s.at[q - 2, 0], h_r.at[q - 2, 0], at_z(-1)),
            remote(sbuf.at[at - 1], hbuf.at[q - 2, 1], h_s.at[q - 2, 1], h_r.at[q - 2, 1], at_z(1)),
        ]
        return made, copies

    def pair_home(q, state):
        made, copies = state
        for side, at in ((0, 4 * q + 1), (1, 4 * q)):
            copies[side].wait_recv()
            sbuf[at - 1] = (made[at - 4 * q] + hbuf[q - 2, side].astype(F32)).astype(BF)
            home(at, -((at + 1) // 2) if side == 0 else at // 2)

    scope = jax.named_scope
    with scope("hop2"):
        landed(2)
        hop(3)
    landed(1)
    with scope("pick0"):
        sent0 = pick(0)
    with scope("hop3"):
        landed(3)
        hop(4)
    with scope("spread0"):
        q0 = spread(0, sent0)
    with scope("hop4"):
        landed(4)
        hop(5)
    with scope("pick1"):
        sent1 = pick(1)
    with scope("hop5"):
        landed(5)
        hop(6)
    with scope("spread1"):
        q1 = spread(1, sent1)
    with scope("hop6"):
        landed(6)
        hop(7)
    with scope("pick2"):
        sent2 = pick(2)
    with scope("hop7"):
        landed(7)
        hop(8)
    with scope("forward0"):
        q0 = forward(0, q0)
    with scope("spread2"):
        q2 = spread(2, sent2)
    with scope("hop8"):
        landed(8)
    with scope("pick3"):
        sent3 = pick(3)
    with scope("forward1"):
        q1 = forward(1, q1)
    with scope("last0"):
        q0 = last(0, q0)
    with scope("loads"):
        for load in loads:
            load.wait()
    with scope("c0"):
        c0 = compute(0, q0)
    with scope("s3"):
        q3 = spread(3, sent3)
    with scope("f2"):
        q2 = forward(2, q2)
    with scope("l1"):
        q1 = last(1, q1)
    with scope("c1"):
        c1 = compute(1, q1)
    with scope("f3"):
        q3 = forward(3, q3)
    with scope("a0"):
        b0 = back_first(0, c0)
    with scope("a1"):
        b1 = back_first(1, c1)
    with scope("l2"):
        q2 = last(2, q2)
    with scope("c2"):
        c2 = compute(2, q2)
    with scope("b0"):
        b0 = back_second(0, b0)
    with scope("l3"):
        q3 = last(3, q3)
    with scope("b1"):
        b1 = back_second(1, b1)
    with scope("a2"):
        b2 = back_first(2, c2)
    with scope("c3"):
        c3 = compute(3, q3)
    with scope("y0"):
        y0 = back_y(0, b0)
    with scope("a3"):
        b3 = back_first(3, c3)
    with scope("b2"):
        b2 = back_second(2, b2)
    with scope("y1"):
        y1 = back_y(1, b1)
    with scope("h0"):
        near_home(0, y0)
    with scope("b3"):
        b3 = back_second(3, b3)
    with scope("h1"):
        near_home(1, y1)
    with scope("w00"):
        weight_grads(0, 0)
    with scope("y2"):
        y2 = back_y(2, b2)
    with scope("w01"):
        weight_grads(0, 1)
    with scope("p2"):
        p2 = pair_start(2, y2)
    with scope("y3"):
        y3 = back_y(3, b3)
    with scope("p2b"):
        pair_home(2, p2)
    with scope("p3"):
        p3 = pair_start(3, y3)
    with scope("w10"):
        weight_grads(1, 0)
    with scope("p3b"):
        pair_home(3, p3)
    with scope("w11"):
        weight_grads(1, 1)
    with scope("finish"):
        total = part[...]
        for k, copy in enumerate(into):
            copy.wait_recv()
            total = total + nbuf[k].astype(F32)
        gtok_ref[:, :HALF] = total[0:8].astype(BF)
        gtok_ref[:, HALF:] = total[8:16].astype(BF)
        for copy in started:
            copy.wait_send()


def write_out(a_ref, b_ref, c_ref, a_out, b_out, c_out, sem):
    pairs = ((a_ref, a_out), (b_ref, b_out), (c_ref, c_out))
    copies = [pltpu.make_async_copy(i, o, sem.at[k]) for k, (i, o) in enumerate(pairs)]
    for copy in copies:
        copy.start()
    for copy in copies:
        copy.wait()


def shards(tokens, out_grad, ids, gates, w_gate, w_up, w_down):
    vmem = pl.BlockSpec(memory_space=pltpu.VMEM)
    hbm = pl.BlockSpec(memory_space=pltpu.HBM)
    dma = pltpu.SemaphoreType.DMA
    three = [dma((4, 3)), dma((4, 3))]
    four = [dma((4, 4)), dma((4, 4))]
    made = pl.pallas_call(
        kernel,
        out_shape=(
            jax.ShapeDtypeStruct((TOK, D), BF),
            pltpu.VMEM((D, HID), F32),
            pltpu.VMEM((D, HID), F32),
            pltpu.VMEM((HID, D), F32),
        ),
        in_specs=[hbm] * 2 + [vmem] * 2 + [hbm] * 3,
        out_specs=(vmem,) * 4,
        scratch_shapes=[
            pltpu.VMEM((TOK, TOP), I32),
            pltpu.VMEM((TOK, TOP), F32),
            pltpu.VMEM((NZ, 8, 128), F32),
            pltpu.VMEM((4, 128, 128), F32),
            pltpu.VMEM((NZ, 16, D), BF),
            pltpu.VMEM((4, 32, 64), F32),
            pltpu.VMEM((4, 3, 16, D), BF),
            pltpu.VMEM((4, NY, 16, D), BF),
            pltpu.VMEM((4, 2, NX, 2, 32, D), BF),
            pltpu.VMEM((D, 2 * HID), BF),
            pltpu.VMEM((HID, D), BF),
            pltpu.VMEM((4, 256, 2 * HID), BF),
            pltpu.VMEM((4, 256, HID), BF),
            pltpu.VMEM((4, NX, 2, 32, D), BF),
            pltpu.VMEM((4, NX, 32, D), BF),
            pltpu.VMEM((4, 3, 32, D), BF),
            pltpu.VMEM((4, 2, 16, D), BF),
            pltpu.VMEM((4, 2, 32, D), BF),
            pltpu.VMEM((4, 3, 16, HALF), BF),
            pltpu.VMEM((4, NY, 16, HALF), BF),
            pltpu.VMEM((16, HALF), F32),
            pltpu.VMEM((15, 16, HALF), BF),
            pltpu.VMEM((11, 16, HALF), BF),
            pltpu.VMEM((2, 2, 16, HALF), BF),
            dma((5,)),
            dma((NZ,)), dma((NZ,)), dma((NZ,)), dma((NZ,)),
            *three, *four, *four, *four,
            dma((4, 2)), dma((4, 2)), *four, *three,
            dma((11,)), dma((11,)), dma((2, 2)), dma((2, 2)),
        ],
        compiler_params=pltpu.CompilerParams(
            collective_id=0, has_side_effects=True, vmem_limit_bytes=52 * 2**20
        ),
    )(ids, gates, tokens, out_grad, w_gate[0], w_up[0], w_down[0])
    gg, gu, gd = pl.pallas_call(
        write_out,
        out_shape=tuple(jax.ShapeDtypeStruct(a.shape, a.dtype) for a in made[1:]),
        in_specs=[vmem] * 3,
        out_specs=(pl.BlockSpec(memory_space=pltpu.HBM),) * 3,
        scratch_shapes=[dma((3,))],
    )(*(pltpu.with_memory_space_constraint(a, pltpu.VMEM) for a in made[1:]))
    return made[0], gg[None], gu[None], gd[None]


def solution(mesh):
    tok = P(("dp", "expert"), None)
    col, row = P("expert", None, "dp"), P("expert", "dp", None)
    return jax.shard_map(
        shards,
        mesh=mesh,
        in_specs=(tok, tok, tok, tok, col, col, row),
        out_specs=(tok, col, col, row),
        check_vma=False,
    )
```
